32 devices in a mesh: cuts: 2 (over x), outer: 16 (over z, y, core).
Axes of the slice: x: 2, y: 2, z: 4, core: 2. Of those that a mesh axis runs over, the one named last changes fastest.
Arguments:
- stem_tensor: bfloat16 [32, 512, 2, 512], P(('cuts', 'outer')), parts along dimension 0, may hold values from -6 to 6
- leaf_left: bfloat16 [4, 2, 8192, 2, 512], P(None, None, 'outer'), may hold values from -0.09375 to 0.09375
- leaf_right: bfloat16 [4, 2, 8192, 2, 512], P(None, None, 'outer'), may hold values from -0.125 to 0.125
- slice_bits: int32 [8], P('cuts'), parts along dimension 0, may hold values from 0 to 1, as said below
Outputs:
- stem_out: bfloat16 [32, 512, 2, 512], P(('cuts', 'outer')), parts along dimension 0
The draws below stay inside these ranges and needn't reach their ends.
There are 2 independent parts, one for each index of `cuts`. The reference program is written for one: setup_inputs(seed, part) draws one part's arguments, and reference() takes and returns one part's arrays. A program takes and returns all parts, laid end to end along the dimension named above; an argument that names none is the same for every part. Nothing has to cross between parts.
Inputs may be any that keep to these rules, and one draw needn't show every extreme that they name: `slice_bits`: the first entry is the index of the part modulo 2, so neighbouring parts contract different slices; the other entries are drawn independently.
All inputs are finite; a program needn't handle non-finite values.
Results may differ from the reference program's by a relative error of at most 0.01.
Values may be sent and summed in bfloat16 or wider, within the bound.
No kernel may reach another device: no remote copies, remote signals or barrier semaphores. Data moves between devices by JAX's collectives and lax.ppermute only.
A program may use at most 64 MiB of HBM per device.

```python
import jax
import jax.numpy as jnp
from jax import lax

W = 512
K = 8192
ROUNDS = 2
SLICES = 2
BR = 4
SHARDS = 16


def draw_slice_bits(key, part):
    drawn = jax.random.randint(key, (BR,), 0, 2, dtype=jnp.int32)
    first = jnp.asarray(part, jnp.int32) % 2
    return drawn.at[0].set(first)


def with_spikes(entries, own_key, source, target, blocks, factor):
    def block_of(axis_at):
        return (jnp.arange(entries.shape[axis_at]) // (entries.shape[axis_at] // blocks)).reshape((-1,) + (1,) * (entries.ndim - 1 - axis_at))

    one_side = jax.random.permutation(own_key, blocks)[block_of(target)]
    other_side = (block_of(target) + blocks // 2) % blocks
    return jnp.where((block_of(source) == one_side) | (block_of(source) == other_side), factor * entries, entries)


def levels(key, dims, pieces, low, largest):
    gain, own = 1.0, jax.random.fold_in(key, 6)
    for dim, blocks in pieces:
        steps = jnp.exp(jax.random.uniform(jax.random.fold_in(own, dim), (blocks,), jnp.float32, low / len(pieces), largest / len(pieces)))
        gain = gain * jnp.repeat(steps, dims[dim] // blocks).reshape([-1 if axis == dim else 1 for axis in range(len(dims))])
    return gain


def gaussian(stream_key, extent, scale, reach, cuts=(), kind=jnp.bfloat16):
    values = scale * jax.random.normal(stream_key, extent, jnp.float32)
    if cuts:
        values = values * levels(stream_key, extent, cuts, -0.22, 0.18)
    return jnp.clip(values, -reach, reach).astype(kind)


def bell_draw_with(own_key, shape, width, most, cuts, heavy, kind=jnp.bfloat16):
    values = width * jax.random.normal(own_key, shape, jnp.float32)
    if cuts:
        values = values * levels(own_key, shape, cuts, -0.22, 0.18)
    return jnp.clip(with_spikes(values, jax.random.fold_in(own_key, 3), *heavy), -most, most).astype(kind)


def setup_inputs(seed: int = 0, part: int = 0) -> dict:
    keys = jax.random.split(jax.random.key(seed), 5)
    part_splits = jax.random.split(jax.random.fold_in(keys[4], part), 5)
    stem_tensor = gaussian(part_splits[0], (SHARDS, W, 2, W), 1.0, 6.0, ((0, 16),))
    leaf_left = bell_draw_with(keys[1], (BR, SLICES, K, 2, W), K ** -0.5, 0.09375, ((2, 16),), (2, 4, 16, 2.0))
    leaf_right = gaussian(keys[2], (BR, SLICES, K, 2, W), (4 * W) ** -0.5, 0.125, ((2, 16),))
    slice_bits = draw_slice_bits(jax.random.fold_in(jax.random.fold_in(keys[4], part), 71), part)
    return {"stem_tensor": stem_tensor, "leaf_left": leaf_left, "leaf_right": leaf_right, "slice_bits": slice_bits}


def complex_leaves(left_leaf, right_leaf):
    product = jnp.einsum('kpi,kqm->piqm', left_leaf, right_leaf)
    real_part = product[0, :, 0] - product[1, :, 1]
    imag_part = product[0, :, 1] + product[1, :, 0]
    return jnp.stack([real_part, imag_part], axis=1)


def reference(stem_tensor, leaf_left, leaf_right, slice_bits):
    branches = []
    for branch_index in range(2 * ROUNDS):
        chosen = slice_bits[branch_index].astype(jnp.int32)
        left_leaf = lax.dynamic_index_in_dim(leaf_left[branch_index], chosen, 0, keepdims=False).astype(jnp.float32)
        right_leaf = lax.dynamic_index_in_dim(leaf_right[branch_index], chosen, 0, keepdims=False).astype(jnp.float32)
        branches.append(complex_leaves(left_leaf, right_leaf).astype(jnp.bfloat16))
    shards = SHARDS
    span = W // SHARDS
    state = stem_tensor
    for round_index in range(ROUNDS):
        p_branch = branches[2 * round_index].astype(jnp.float32)
        q_branch = branches[2 * round_index + 1].astype(jnp.float32)
        current = state.astype(jnp.float32)
        product = jnp.einsum('abpc,cqm->abpqm', current, q_branch)
        real_part = product[:, :, 0, 0] - product[:, :, 1, 1]
        imag_part = product[:, :, 0, 1] + product[:, :, 1, 0]
        absorbed = jnp.stack([real_part, imag_part], axis=2).astype(jnp.bfloat16)
        grouped = absorbed.astype(jnp.float32).reshape(shards, shards, span, 2, W)
        p_grouped = p_branch.reshape(shards, span, 2, W)
        product = jnp.einsum('ahlpm,alqn->hnpqm', grouped, p_grouped)
        real_part = product[:, :, 0, 0] - product[:, :, 1, 1]
        imag_part = product[:, :, 0, 1] + product[:, :, 1, 0]
        state = jnp.stack([real_part, imag_part], axis=2).astype(jnp.bfloat16)
    return state
```

```python
import functools

import jax
import jax.numpy as jnp
from jax import lax
from jax.experimental import pallas as pl
from jax.experimental.pallas import tpu as pltpu
from jax.sharding import PartitionSpec as P

ROUNDS = 2
GROUPS = ((0,), (2,), (1,), (3,))
VMEM_LIMIT = 48 << 20
bf16, f32 = jnp.bfloat16, jnp.float32

SMEM_SPEC = pl.BlockSpec(memory_space=pltpu.SMEM)
VMEM_SPEC = pl.BlockSpec(memory_space=pltpu.VMEM)
ANY_SPEC = pl.BlockSpec(memory_space=pl.ANY)


def call(body, out_shape, in_specs, scratch=(), flops=0, moved=0):
    return pl.pallas_call(
        body,
        out_shape=out_shape,
        in_specs=in_specs,
        out_specs=jax.tree.map(lambda _: VMEM_SPEC, out_shape),
        scratch_shapes=list(scratch),
        compiler_params=pltpu.CompilerParams(vmem_limit_bytes=VMEM_LIMIT),
        cost_estimate=pl.CostEstimate(flops=flops, bytes_accessed=moved, transcendentals=0),
    )


def tdot(a, b):
    return lax.dot_general(a, b, (((0,), (0,)), ((), ())), preferred_element_type=f32)


def dot(a, b):
    return jnp.dot(a, b, preferred_element_type=f32)


def leaf_body(branches, meta, left, right, keep, send, lhs, rhs, both, sems):
    depth, width = left.shape[2], left.shape[4]
    core = meta[0] & 1
    copies = []
    for at, j in enumerate(branches):
        first, second = (right, left) if j % 2 == 0 else (left, right)
        for which, (ref, buf) in enumerate(((first, lhs), (second, rhs))):
            flat = ref.reshape(ref.shape[0], ref.shape[1], 2 * depth, width)
            copy = pltpu.make_async_copy(flat.at[j, meta[1 + j]], buf.at[at], sems.at[at, which])
            copy.start()
            copies.append(copy)
    rows = lax.broadcasted_iota(jnp.int32, (2 * depth // 8, 8, width), 1)
    is_real = (rows & 1) == 0
    for at in range(len(branches)):
        copies[2 * at + 1].wait()
        wide = rhs[at].astype(f32).reshape(2 * depth // 8, 8, width)
        signed = jnp.where(is_real, wide, -wide)
        swapped = jnp.where(is_real, pltpu.roll(wide, 7, 1), pltpu.roll(wide, 1, 1))
        both[core] = signed.reshape(2 * depth, width).astype(bf16)
        both[1 - core] = swapped.reshape(2 * depth, width).astype(bf16)
        copies[2 * at].wait()
        send[at] = tdot(lhs[at], both[1]).astype(bf16)
        keep[at] = tdot(lhs[at], both[0])


def leaf_partials(meta, left, right, branches):
    count, depth, width = len(branches), left.shape[2], left.shape[4]
    shape = (count, width, width)
    return call(
        functools.partial(leaf_body, branches),
        (jax.ShapeDtypeStruct(shape, f32), jax.ShapeDtypeStruct(shape, bf16)),
        [SMEM_SPEC, ANY_SPEC, ANY_SPEC],
        [
            pltpu.VMEM((count, 2 * depth, width), bf16),
            pltpu.VMEM((count, 2 * depth, width), bf16),
            pltpu.VMEM((2, 2 * depth, width), bf16),
            pltpu.SemaphoreType.DMA((count, 2)),
        ],
        flops=count * 8 * depth * width * width,
        moved=count * 8 * depth * width,
    )(meta, left, right)


def add_body(shift, meta, keep, recv, keep_out, send_out):
    half = keep_out.shape[1]
    bit = (meta[0] >> shift) & 1
    mine = pl.multiple_of(bit * half, half)
    other = pl.multiple_of((1 - bit) * half, half)
    send_out[...] = (keep[:, pl.ds(other, half)] + recv[:, pl.ds(other, half)].astype(f32)).astype(bf16)
    keep_out[...] = keep[:, pl.ds(mine, half)] + recv[:, pl.ds(mine, half)].astype(f32)


def add_and_split(meta, keep, recv, shift):
    count, rows, width = keep.shape
    half = rows // 2
    if half % 16:
        total = (keep + recv.astype(f32)).reshape(count, 2, half, width)
        bit = (meta[0] >> shift) & 1
        return (
            lax.dynamic_index_in_dim(total, bit, 1, keepdims=False),
            lax.dynamic_index_in_dim(total, 1 - bit, 1, keepdims=False).astype(bf16),
        )
    shape = (count, half, width)
    return call(
        functools.partial(add_body, shift),
        (jax.ShapeDtypeStruct(shape, f32), jax.ShapeDtypeStruct(shape, bf16)),
        [SMEM_SPEC, VMEM_SPEC, VMEM_SPEC],
        moved=count * rows * width * 9,
    )(meta, keep, recv)


def swap_with(x, mask, size):
    return lax.ppermute(x, "outer", [(i, i ^ mask) for i in range(size)])


def full_sum(meta, left, right, branches, size):
    levels = size.bit_length() - 1
    keep, send = leaf_partials(meta, left, right, branches)
    recv = swap_with(send, 1, size)
    for shift in range(1, levels):
        keep, send = add_and_split(meta, keep, recv, shift)
        recv = swap_with(send, 1 << shift, size)
    total = (keep + recv.astype(f32)).astype(bf16)[None]
    for shift in reversed(range(1, levels)):
        total = jnp.concatenate([total, swap_with(total, 1 << shift, size)], axis=0)
    other = swap_with(total, 1, size)
    return total, other


def in_order(meta, planes, at):
    own, other = planes[0][:, at], planes[1][:, at]
    blocks, rows, width = own.shape
    if rows % 16:
        order = block_of(meta, blocks) ^ jnp.arange(blocks)
        own, other = (x[order].reshape(1, blocks * rows, width) for x in (own, other))
    return own, other


def block_of(meta, blocks):
    place, found, shift = meta[0] >> 1, 0, blocks >> 1
    while shift:
        found = found + (place & 1) * shift
        place, shift = place >> 1, shift >> 1
    return found


def prepare_body(meta, stem, out, wide):
    count, width = stem.shape[0], stem.shape[2]
    core = meta[0] & 1
    flat = stem[...].reshape(2 * count, width)
    for at in range(width // 128):
        wide[at] = flat[:, at * 128 : (at + 1) * 128].astype(f32)
    for at in range(width // 128):
        here = slice(at * 128, (at + 1) * 128)
        there = slice(width + at * 128, width + (at + 1) * 128)
        real = wide[at, pl.ds(0, count, stride=2), :]
        imag = wide[at, pl.ds(1, count, stride=2), :]
        out[core, :, here] = real.astype(bf16)
        out[core, :, there] = imag.astype(bf16)
        out[1 - core, :, here] = (-imag).astype(bf16)
        out[1 - core, :, there] = real.astype(bf16)


def prepare(meta, stem):
    count, _, width = stem.shape
    return call(
        prepare_body,
        jax.ShapeDtypeStruct((2, count, 2 * width), bf16),
        [SMEM_SPEC, VMEM_SPEC],
        [pltpu.VMEM((width // 128, 2 * count, 128), f32)],
        moved=6 * count * width * 2,
    )(meta, stem)


def first_body(meta, own, other, right, out):
    blocks, rows, width = own.shape
    me = block_of(meta, blocks)
    mine = own[...].reshape(blocks * rows, width)
    theirs = other[...].reshape(blocks * rows, width)
    tile = 256
    for at in range(right.shape[2] // tile):
        here = slice(at * tile, (at + 1) * tile)
        value = dot(mine, right[0, :, here]) + dot(theirs, right[1, :, here])
        value = value.astype(bf16).reshape(blocks, rows, tile)
        for t in range(blocks):
            out[me ^ t, :, here] = value[t]


def first_product(meta, own, other, right):
    blocks, rows, width = own.shape
    return call(
        first_body,
        jax.ShapeDtypeStruct((blocks, rows, right.shape[2]), bf16),
        [SMEM_SPEC] + [VMEM_SPEC] * 3,
        flops=8 * blocks * rows * width * width,
        moved=10 * width * width,
    )(meta, own, other, right)


def joined_body(meta, own0, other0, own1, other1, out, right):
    blocks, rows, width = own0.shape
    me = block_of(meta, blocks)
    core = meta[0] & 1
    for t in range(blocks):
        own, other = own1[t], other1[t]
        real = jnp.where(core == 0, own, other)
        imag = jnp.where(core == 0, other, own)
        right[core, me ^ t, :, :width] = real
        right[core, me ^ t, :, width:] = imag
        right[1 - core, me ^ t, :, :width] = -imag
        right[1 - core, me ^ t, :, width:] = real
    mine = own0[...].reshape(blocks * rows, width)
    theirs = other0[...].reshape(blocks * rows, width)
    tile = 256
    for at in range(2 * width // tile):
        here = slice(at * tile, (at + 1) * tile)
        there = slice((at * tile + width) % (2 * width), (at * tile + width) % (2 * width) + tile)
        first = right[0, :, :, here].reshape(blocks * rows, tile)
        second = right[1, :, :, here].reshape(blocks * rows, tile)
        value = dot(mine, first) + dot(theirs, second)
        turned = value if at * tile < width else -value
        value = value.astype(bf16).reshape(blocks, rows, tile)
        turned = turned.astype(bf16).reshape(blocks, rows, tile)
        for t in range(blocks):
            out[0, me ^ t, :, here] = value[t]
            out[1, me ^ t, :, there] = turned[t]


def joined_right(meta, own0, other0, own1, other1):
    blocks, rows, width = own0.shape
    return call(
        joined_body,
        jax.ShapeDtypeStruct((2, blocks, rows, 2 * width), bf16),
        [SMEM_SPEC] + [VMEM_SPEC] * 4,
        [pltpu.VMEM((2, blocks, rows, 2 * width), bf16)],
        flops=8 * blocks * rows * width * width,
        moved=16 * width * width,
    )(meta, own0, other0, own1, other1)


def last_body(meta, own, other, stem, factor, out, right, middle, wide, sem):
    blocks, rows, width = own.shape
    total = blocks * rows
    count = stem.shape[0]
    me = block_of(meta, blocks)
    core = meta[0] & 1
    right[core] = stem[...]
    right[1 - core, :, :width] = -stem[:, width:]
    right[1 - core, :, width:] = stem[:, :width]
    mine = own[...].reshape(total, width)
    theirs = other[...].reshape(total, width)
    tile = 256
    for at in range(2 * width // tile):
        here = slice(at * tile, (at + 1) * tile)
        middle[:, here] = (dot(mine, right[0, :, here]) + dot(theirs, right[1, :, here])).astype(bf16)
    for at in range(width // tile):
        for part in range(2):
            here = slice(part * width + at * tile, part * width + (at + 1) * tile)
            value = dot(middle[:, :width], factor[0, :, here]) + dot(middle[:, width:], factor[1, :, here])
            for sub in range(tile // 128):
                wide[at * (tile // 128) + sub, pl.ds(part, total, stride=2), :] = value[:, sub * 128 : (sub + 1) * 128]
    for at in range(width // 128):
        for t in range(blocks):
            piece = wide[at, 2 * rows * t : 2 * rows * (t + 1), :]
            out[me ^ t, :, at * 128 : (at + 1) * 128] = piece.astype(bf16)


def last_product(meta, own, other, stem, factor):
    blocks, rows, width = own.shape
    count = stem.shape[0]
    return call(
        last_body,
        jax.ShapeDtypeStruct((blocks, 2 * rows, width), bf16),
        [SMEM_SPEC] + [VMEM_SPEC] * 4,
        [
            pltpu.VMEM((2, count, 2 * width), bf16),
            pltpu.VMEM((blocks * rows, 2 * width), bf16),
            pltpu.VMEM((width // 128, 2 * blocks * rows, 128), f32),
            pltpu.SemaphoreType.DMA,
        ],
        flops=16 * blocks * rows * width * width,
        moved=20 * width * width,
    )(meta, own, other, stem, factor)


def on_device(size, stem_tensor, leaf_left, leaf_right, slice_bits):
    width = stem_tensor.shape[1]
    place = lax.axis_index("outer").astype(jnp.int32)
    meta = jnp.concatenate([place[None], slice_bits.astype(jnp.int32)])
    sums = {}
    for branches in GROUPS:
        planes = full_sum(meta, leaf_left, leaf_right, branches, size)
        for at, j in enumerate(branches):
            sums[j] = in_order(meta, planes, at)
    spread = lax.all_to_all(stem_tensor[0], "outer", split_axis=0, concat_axis=0, tiled=True)
    right = prepare(meta, spread)
    state = first_product(meta, *sums[0], right).reshape(width, 2 * width)
    state = lax.all_to_all(state, "outer", split_axis=0, concat_axis=0, tiled=True)
    factor = joined_right(meta, *sums[1], *sums[3]).reshape(2, width, 2 * width)
    result = last_product(meta, *sums[2], state, factor)
    return result.reshape(stem_tensor.shape)


def solution(mesh):
    return jax.shard_map(
        functools.partial(on_device, mesh.shape["outer"]),
        mesh=mesh,
        in_specs=(
            P(("cuts", "outer"), None, None, None),
            P(None, None, "outer", None, None),
            P(None, None, "outer", None, None),
            P("cuts"),
        ),
        out_specs=P(("cuts", "outer"), None, None, None),
        check_vma=False,
    )
```

```python
import functools

import jax
import jax.numpy as jnp
from jax import lax
from jax.experimental import pallas as pl
from jax.experimental.pallas import tpu as pltpu
from jax.sharding import PartitionSpec as P

VMEM_LIMIT = 48 << 20
TILE = 256
bf16, f32 = jnp.bfloat16, jnp.float32

SMEM_SPEC = pl.BlockSpec(memory_space=pltpu.SMEM)
VMEM_SPEC = pl.BlockSpec(memory_space=pltpu.VMEM)
ANY_SPEC = pl.BlockSpec(memory_space=pl.ANY)


class Chain:
    def __init__(self, meta):
        self.meta, self.last = meta, None

    def __call__(self, body, shapes, in_specs, operands, scratch=(), out_specs=None):
        many = isinstance(shapes, (tuple, list))
        shapes = tuple(shapes) if many else (shapes,)
        specs, extra = [SMEM_SPEC] + list(in_specs), []
        if self.last is not None:
            specs, extra = specs + [ANY_SPEC], [self.last]
        count = len(specs)

        def kernel(*refs):
            body(*refs[: len(in_specs) + 1], *refs[count:])

        out = pl.pallas_call(
            kernel,
            out_shape=shapes,
            in_specs=specs,
            out_specs=tuple(out_specs or [VMEM_SPEC] * len(shapes)),
            scratch_shapes=list(scratch),
            compiler_params=pltpu.CompilerParams(vmem_limit_bytes=VMEM_LIMIT),
            cost_estimate=pl.CostEstimate(flops=0, bytes_accessed=1024, transcendentals=0),
        )(self.meta, *operands, *extra)
        self.last = out[0]
        return out if many else out[0]


def shaped(shape, dtype=bf16):
    return jax.ShapeDtypeStruct(shape, dtype)


def tdot(a, b):
    return lax.dot_general(a, b, (((0,), (0,)), ((), ())), preferred_element_type=f32)


def dot(a, b):
    return jnp.dot(a, b, preferred_element_type=f32)


def reversed_bits(value, bits):
    found = 0
    for at in range(bits):
        found = found + ((value >> at) & 1) * (1 << (bits - 1 - at))
    return found


def block_of(meta, blocks):
    return reversed_bits(meta[0] >> 1, blocks.bit_length() - 1)


def leaf_body(branch, meta, left, right, keep, send, lhs, rhs, both, sems):
    depth, width = left.shape[2], left.shape[4]
    core = meta[0] & 1
    first, second = (right, left) if branch % 2 == 0 else (left, right)
    copies = []
    for which, (ref, buf) in enumerate(((second, rhs), (first, lhs))):
        flat = ref.reshape(ref.shape[0], ref.shape[1], 2 * depth, width)
        copies.append(pltpu.make_async_copy(flat.at[branch, meta[1 + branch]], buf, sems.at[which]))
        copies[-1].start()
    rows = lax.broadcasted_iota(jnp.int32, (2 * depth // 8, 8, width), 1)
    is_real = (rows & 1) == 0
    copies[0].wait()
    wide = rhs[...].astype(f32).reshape(2 * depth // 8, 8, width)
    signed = jnp.where(is_real, wide, -wide)
    swapped = jnp.where(is_real, pltpu.roll(wide, 7, 1), pltpu.roll(wide, 1, 1))
    both[core] = signed.reshape(2 * depth, width).astype(bf16)
    both[1 - core] = swapped.reshape(2 * depth, width).astype(bf16)
    copies[1].wait()
    send[...] = tdot(lhs[...], both[1]).astype(bf16)
    keep[...] = tdot(lhs[...], both[0])


def leaf_partial(chain, left, right, branch):
    depth, width = left.shape[2], left.shape[4]
    return chain(
        functools.partial(leaf_body, branch),
        (shaped((width, width), f32), shaped((width, width))),
        [ANY_SPEC, ANY_SPEC],
        (left, right),
        [
            pltpu.VMEM((2 * depth, width), bf16),
            pltpu.VMEM((2 * depth, width), bf16),
            pltpu.VMEM((2, 2 * depth, width), bf16),
            pltpu.SemaphoreType.DMA((2,)),
        ],
    )


def half_body(shift, meta, keep, recv, keep_out, send_out):
    half = keep_out.shape[0]
    bit = (meta[0] >> shift) & 1
    mine = pl.multiple_of(bit * half, half)
    other = pl.multiple_of((1 - bit) * half, half)
    send_out[...] = (keep[pl.ds(other, half)] + recv[pl.ds(other, half)].astype(f32)).astype(bf16)
    keep_out[...] = keep[pl.ds(mine, half)] + recv[pl.ds(mine, half)].astype(f32)


def halve(chain, keep, recv, shift):
    rows, width = keep.shape
    half = rows // 2
    if half % 16:
        total = (keep + recv.astype(f32)).reshape(2, half, width)
        bit = (chain.meta[0] >> shift) & 1
        return total[bit], total[1 - bit].astype(bf16)
    return chain(
        functools.partial(half_body, shift),
        (shaped((half, width), f32), shaped((half, width))),
        [VMEM_SPEC] * 2,
        (keep, recv),
    )


def spread_body(shift, meta, keep, recv, keep_out, *sends):
    rows = keep_out.shape[0]
    blocks = len(sends) + 1
    me = reversed_bits(meta[0] >> shift, blocks.bit_length() - 1)
    for t in range(blocks):
        at = pl.ds(pl.multiple_of((me ^ t) * rows, rows), rows)
        value = keep[at] + recv[at].astype(f32)
        if t:
            sends[t - 1][...] = value.astype(bf16)
        else:
            keep_out[...] = value


def spread(chain, keep, recv, shift, blocks):
    rows, width = keep.shape[0] // blocks, keep.shape[1]
    return chain(
        functools.partial(spread_body, shift),
        (shaped((rows, width), f32),) + (shaped((rows, width)),) * (blocks - 1),
        [VMEM_SPEC] * 2,
        (keep, recv),
    )


def finish_body(meta, keep, *rest):
    total = keep[...]
    for recv in rest[:-1]:
        total = total + recv[...].astype(f32)
    rest[-1][0] = total.astype(bf16)


def finish(chain, keep, recvs):
    rows, width = keep.shape
    if rows % 16:
        return (keep + sum(recv.astype(f32) for recv in recvs)).astype(bf16)[None]
    return chain(finish_body, shaped((1, rows, width)), [VMEM_SPEC] * (1 + len(recvs)), (keep, *recvs))


def join_body(meta, *refs):
    at = 0
    for ref in refs[:-1]:
        refs[-1][at : at + ref.shape[0]] = ref[...]
        at += ref.shape[0]


def join(chain, parts):
    blocks, rows, width = sum(part.shape[0] for part in parts), *parts[0].shape[1:]
    if rows % 16:
        return jnp.concatenate(parts, axis=0)
    return chain(join_body, shaped((blocks, rows, width)), [VMEM_SPEC] * len(parts), parts)


def swap_with(x, mask, size):
    return lax.ppermute(x, "outer", [(i, i ^ mask) for i in range(size)])


def prepare_body(meta, stem, out, wide):
    count, width = stem.shape[0], stem.shape[2]
    core = meta[0] & 1
    flat = stem[...].reshape(2 * count, width)
    for at in range(width // 128):
        wide[at] = flat[:, at * 128 : (at + 1) * 128].astype(f32)
    for at in range(width // 128):
        here = slice(at * 128, (at + 1) * 128)
        there = slice(width + at * 128, width + (at + 1) * 128)
        real = wide[at, pl.ds(0, count, stride=2), :]
        imag = wide[at, pl.ds(1, count, stride=2), :]
        out[core, :, here] = real.astype(bf16)
        out[core, :, there] = imag.astype(bf16)
        out[1 - core, :, here] = (-imag).astype(bf16)
        out[1 - core, :, there] = real.astype(bf16)


def prepare(chain, stem):
    count, _, width = stem.shape
    return chain(
        prepare_body,
        shaped((2, count, 2 * width)),
        [VMEM_SPEC],
        (stem,),
        [pltpu.VMEM((width // 128, 2 * count, 128), f32)],
    )


def rows_of(refs, width):
    return jnp.concatenate([ref[...].reshape(-1, width) for ref in refs], axis=0)


def layout(planes):
    return sum(part.shape[0] for part in planes), *planes[0].shape[1:]


def first_body(parts, meta, *refs):
    own, other, (right, out) = refs[:parts], refs[parts : 2 * parts], refs[2 * parts :]
    blocks, rows, columns = out.shape
    me = block_of(meta, blocks)
    mine, theirs = rows_of(own, columns // 2), rows_of(other, columns // 2)
    for at in range(columns // TILE):
        here = slice(at * TILE, (at + 1) * TILE)
        value = dot(mine, right[0, :, here]) + dot(theirs, right[1, :, here])
        value = value.astype(bf16).reshape(blocks, rows, TILE)
        for t in range(blocks):
            out[me ^ t, :, here] = value[t]


def first_product(chain, branch, right):
    own, other = branch
    blocks, rows, width = layout(own)
    return chain(
        functools.partial(first_body, len(own)),
        shaped((blocks, rows, 2 * width)),
        [VMEM_SPEC] * (2 * len(own) + 1),
        (*own, *other, right),
    )


def joined_body(parts, meta, *refs):
    own0, other0, own1, other1 = (refs[at * parts : (at + 1) * parts] for at in range(4))
    out, right = refs[4 * parts :]
    _, blocks, rows, columns = out.shape
    width = columns // 2
    me = block_of(meta, blocks)
    core = meta[0] & 1
    t = 0
    for own_ref, other_ref in zip(own1, other1, strict=True):
        for at in range(own_ref.shape[0]):
            own, other = own_ref[at], other_ref[at]
            real = jnp.where(core == 0, own, other)
            imag = jnp.where(core == 0, other, own)
            right[core, me ^ t, :, :width] = real
            right[core, me ^ t, :, width:] = imag
            right[1 - core, me ^ t, :, :width] = -imag
            right[1 - core, me ^ t, :, width:] = real
            t += 1
    mine, theirs = rows_of(own0, width), rows_of(other0, width)
    for at in range(columns // TILE):
        here = slice(at * TILE, (at + 1) * TILE)
        there = slice((at * TILE + width) % columns, (at * TILE + width) % columns + TILE)
        first = right[0, :, :, here].reshape(blocks * rows, TILE)
        second = right[1, :, :, here].reshape(blocks * rows, TILE)
        value = dot(mine, first) + dot(theirs, second)
        turned = value if at * TILE < width else -value
        value = value.astype(bf16).reshape(blocks, rows, TILE)
        turned = turned.astype(bf16).reshape(blocks, rows, TILE)
        for t in range(blocks):
            out[0, me ^ t, :, here] = value[t]
            out[1, me ^ t, :, there] = turned[t]


def joined_right(chain, first, second):
    blocks, rows, width = layout(first[0])
    parts = len(first[0])
    return chain(
        functools.partial(joined_body, parts),
        shaped((2, blocks, rows, 2 * width)),
        [VMEM_SPEC] * (4 * parts),
        (*first[0], *first[1], *second[0], *second[1]),
        [pltpu.VMEM((2, blocks, rows, 2 * width), bf16)],
    )


def last_body(parts, meta, *refs):
    own, other = refs[:parts], refs[parts : 2 * parts]
    stem, factor, out, left, given, both, right, middle, wide, done, sems = refs[2 * parts :]
    _, blocks, rows, width = left.shape
    total = blocks * rows
    core = meta[0] & 1
    me = block_of(meta, blocks)
    copies = [pltpu.make_async_copy(stem, given, sems.at[0]), pltpu.make_async_copy(factor, both, sems.at[1])]
    for plane, refs_of in enumerate((own, other)):
        at = 0
        for ref in refs_of:
            size = ref.shape[0]
            copies.append(pltpu.make_async_copy(ref, left.at[plane, pl.ds(at, size)], sems.at[len(copies)]))
            at += size
    for copy in copies:
        copy.start()
    copies[0].wait()
    value = given[...]
    right[core] = value
    right[1 - core, :, :width] = -value[:, width:]
    right[1 - core, :, width:] = value[:, :width]
    for copy in copies[2:]:
        copy.wait()
    mine = left[0].reshape(total, width)
    theirs = left[1].reshape(total, width)
    for at in range(2 * width // TILE):
        here = slice(at * TILE, (at + 1) * TILE)
        middle[:, here] = (dot(mine, right[0, :, here]) + dot(theirs, right[1, :, here])).astype(bf16)
    copies[1].wait()
    for at in range(width // TILE):
        for part in range(2):
            here = slice(part * width + at * TILE, part * width + (at + 1) * TILE)
            value = dot(middle[:, :width], both[0, :, here]) + dot(middle[:, width:], both[1, :, here])
            for sub in range(TILE // 128):
                wide[at * (TILE // 128) + sub, pl.ds(part, total, stride=2), :] = value[:, sub * 128 : (sub + 1) * 128]
    target = out.reshape(blocks, 2 * rows, width)
    writes = []
    for t in range(blocks):
        for at in range(width // 128):
            piece = wide[at, 2 * rows * t : 2 * rows * (t + 1), :]
            done[t, :, at * 128 : (at + 1) * 128] = piece.astype(bf16)
        writes.append(pltpu.make_async_copy(done.at[t], target.at[me ^ t], sems.at[len(copies) + t]))
        writes[-1].start()
    for copy in writes:
        copy.wait()


def last_product(chain, branch, stem, factor, shape):
    own, other = branch
    blocks, rows, width = layout(own)
    count = stem.shape[0]
    return chain(
        functools.partial(last_body, len(own)),
        shaped(shape),
        [ANY_SPEC] * (2 * len(own) + 2),
        (*own, *other, stem, factor),
        [
            pltpu.VMEM((2, blocks, rows, width), bf16),
            pltpu.VMEM((count, 2 * width), bf16),
            pltpu.VMEM((2, width, 2 * width), bf16),
            pltpu.VMEM((2, count, 2 * width), bf16),
            pltpu.VMEM((blocks * rows, 2 * width), bf16),
            pltpu.VMEM((width // 128, 2 * blocks * rows, 128), f32),
            pltpu.VMEM((blocks, 2 * rows, width), bf16),
            pltpu.SemaphoreType.DMA((2 + 2 * len(own) + blocks,)),
        ],
        [ANY_SPEC],
    )


def exchange(x):
    return lax.all_to_all(x, "outer", split_axis=0, concat_axis=0, tiled=True)


class Sum:
    def __init__(self, chain, left, right, branch, size, direct):
        self.chain, self.size, self.direct = chain, size, direct
        self.levels = size.bit_length() - 1
        self.keep, send = leaf_partial(chain, left, right, branch)
        self.recv = self.swap(send, 0)

    def swap(self, x, shift):
        return swap_with(x, 1 << shift, self.size)

    def steps(self):
        levels = self.levels
        direct = 1 << (levels - 2) if self.direct else 1
        stop = 2 if self.direct else levels
        for shift in range(1, stop):
            self.keep, send = halve(self.chain, self.keep, self.recv, shift)
            self.recv = self.swap(send, shift)
            yield
        masks = [reversed_bits(t, levels - 2) << 2 for t in range(1, direct)]
        if self.direct:
            self.keep, *sends = spread(self.chain, self.keep, self.recv, 2, direct)
            recvs = [swap_with(x, mask, self.size) for x, mask in zip(sends, masks, strict=True)]
            yield
        else:
            recvs = [self.recv]
        total = finish(self.chain, self.keep, recvs)
        if self.direct:
            recvs = [swap_with(total, mask, self.size) for mask in masks]
            yield
            total = join(self.chain, (total, *recvs))
        else:
            for shift in reversed(range(2, levels)):
                recv = self.swap(total, shift)
                yield
                total = join(self.chain, (total, recv))
        across = self.swap(total, 1)
        own = (total, across)
        other = (self.swap(total, 0), self.swap(across, 0))
        rows, width = total.shape[1:]
        if rows % 16:
            blocks = 1 << (levels - 1)
            order = block_of(self.chain.meta, blocks) ^ jnp.arange(blocks)
            own, other = (
                (jnp.concatenate(x, axis=0)[order].reshape(1, blocks * rows, width),) for x in (own, other)
            )
        self.result = own, other


def on_device(size, stem_tensor, leaf_left, leaf_right, slice_bits):
    width = stem_tensor.shape[1]
    place = lax.axis_index("outer").astype(jnp.int32)
    chain = Chain(jnp.concatenate([place[None], slice_bits.astype(jnp.int32)]))
    fine = width // size * 2 % 16 == 0
    given = exchange(stem_tensor[0])

    sums, runs = {}, {}

    def begin(j):
        sums[j] = Sum(chain, leaf_left, leaf_right, j, size, fine and j == 0)
        runs[j] = sums[j].steps()

    def step(*order):
        for j in order:
            next(runs[j], None)

    def end(j):
        for _ in runs[j]:
            pass
        return sums[j].result

    begin(0)
    begin(2)
    step(0)
    begin(1)
    step(2)
    begin(3)
    step(0)
    step(1, 3)
    step(0)
    step(2)
    right = prepare(chain, given)
    step(0)
    step(1, 2, 3, 1)
    end(0)
    state = first_product(chain, sums[0].result, right).reshape(width, 2 * width)
    state = exchange(state)
    step(2, 3, 1, 2, 3, 1, 2, 3, 1)
    end(1)
    end(3)
    end(2)
    factor = joined_right(chain, sums[1].result, sums[3].result).reshape(2, width, 2 * width)
    return last_product(chain, sums[2].result, state, factor, stem_tensor.shape)


def solution(mesh):
    return jax.shard_map(
        functools.partial(on_device, mesh.shape["outer"]),
        mesh=mesh,
        in_specs=(
            P(("cuts", "outer"), None, None, None),
            P(None, None, "outer", None, None),
            P(None, None, "outer", None, None),
            P("cuts"),
        ),
        out_specs=P(("cuts", "outer"), None, None, None),
        check_vma=False,
    )
```

```python
import functools

import jax
import jax.numpy as jnp
from jax import lax
from jax.experimental import pallas as pl
from jax.experimental.pallas import tpu as pltpu
from jax.sharding import PartitionSpec as P

VMEM_LIMIT = 24 << 20
TILE = 256
bf16, f32 = jnp.bfloat16, jnp.float32

SMEM_SPEC = pl.BlockSpec(memory_space=pltpu.SMEM)
VMEM_SPEC = pl.BlockSpec(memory_space=pltpu.VMEM)
ANY_SPEC = pl.BlockSpec(memory_space=pl.ANY)


class Chain:
    def __init__(self, meta):
        self.meta, self.last = meta, None

    def __call__(self, body, shapes, in_specs, operands, scratch=(), out_specs=None, us=1.0):
        many = isinstance(shapes, (tuple, list))
        shapes = tuple(shapes) if many else (shapes,)
        specs, extra = [SMEM_SPEC] + list(in_specs), []
        if self.last is not None:
            specs, extra = specs + [ANY_SPEC], [self.last]
        count = len(specs)

        def kernel(*refs):
            body(*refs[: len(in_specs) + 1], *refs[count:])

        out = pl.pallas_call(
            kernel,
            out_shape=shapes,
            in_specs=specs,
            out_specs=tuple(out_specs or [VMEM_SPEC] * len(shapes)),
            scratch_shapes=list(scratch),
            compiler_params=pltpu.CompilerParams(vmem_limit_bytes=VMEM_LIMIT),
            cost_estimate=pl.CostEstimate(flops=int(us * 1e9), bytes_accessed=1024, transcendentals=0),
        )(self.meta, *operands, *extra)
        self.last = out[0]
        return out if many else out[0]


def shaped(shape, dtype=bf16):
    return jax.ShapeDtypeStruct(shape, dtype)


def tdot(a, b):
    return lax.dot_general(a, b, (((0,), (0,)), ((), ())), preferred_element_type=f32)


def dot(a, b):
    return jnp.dot(a, b, preferred_element_type=f32)


def reversed_bits(value, bits):
    found = 0
    for at in range(bits):
        found = found + ((value >> at) & 1) * (1 << (bits - 1 - at))
    return found


def block_of(meta, blocks):
    return reversed_bits(meta[0] >> 1, blocks.bit_length() - 1)


def leaf_body(branch, meta, left, right, keep, send, lhs, rhs, both, sems):
    depth, width = left.shape[2], left.shape[4]
    core = meta[0] & 1
    first, second = (right, left) if branch % 2 == 0 else (left, right)
    copies = []
    for which, (ref, buf) in enumerate(((second, rhs), (first, lhs))):
        flat = ref.reshape(ref.shape[0], ref.shape[1], 2 * depth, width)
        copies.append(pltpu.make_async_copy(flat.at[branch, meta[1 + branch]], buf, sems.at[which]))
        copies[-1].start()
    rows = lax.broadcasted_iota(jnp.int32, (2 * depth // 8, 8, width), 1)
    is_real = (rows & 1) == 0
    copies[0].wait()
    wide = rhs[...].astype(f32).reshape(2 * depth // 8, 8, width)
    signed = jnp.where(is_real, wide, -wide)
    swapped = jnp.where(is_real, pltpu.roll(wide, 7, 1), pltpu.roll(wide, 1, 1))
    both[core] = signed.reshape(2 * depth, width).astype(bf16)
    both[1 - core] = swapped.reshape(2 * depth, width).astype(bf16)
    copies[1].wait()
    send[...] = tdot(lhs[...], both[1]).astype(bf16)
    keep[...] = tdot(lhs[...], both[0])


def leaf_partial(chain, left, right, branch):
    depth, width = left.shape[2], left.shape[4]
    return chain(
        functools.partial(leaf_body, branch),
        (shaped((width, width), f32), shaped((width, width))),
        [ANY_SPEC, ANY_SPEC],
        (left, right),
        [
            pltpu.VMEM((2 * depth, width), bf16),
            pltpu.VMEM((2 * depth, width), bf16),
            pltpu.VMEM((2, 2 * depth, width), bf16),
            pltpu.SemaphoreType.DMA((2,)),
        ],
        us=3.5,
    )


def half_body(count, shift, meta, *refs):
    keeps, recvs, (keep_out, send_out) = refs[:count], refs[count : 2 * count], refs[2 * count :]
    half = keep_out.shape[1]
    bit = (meta[0] >> shift) & 1
    mine = pl.ds(pl.multiple_of(bit * half, half), half)
    other = pl.ds(pl.multiple_of((1 - bit) * half, half), half)
    for at, (keep, recv) in enumerate(zip(keeps, recvs, strict=True)):
        send_out[at] = (keep[other] + recv[other].astype(f32)).astype(bf16)
        keep_out[at] = keep[mine] + recv[mine].astype(f32)


def halve(chain, keeps, recvs, shift):
    count, (rows, width) = len(keeps), keeps[0].shape
    half = rows // 2
    if half % 16:
        total = jnp.stack([keep + recv.astype(f32) for keep, recv in zip(keeps, recvs, strict=True)])
        total = total.reshape(count, 2, half, width)
        bit = (chain.meta[0] >> shift) & 1
        return total[:, bit], total[:, 1 - bit].astype(bf16)
    return chain(
        functools.partial(half_body, count, shift),
        (shaped((count, half, width), f32), shaped((count, half, width))),
        [VMEM_SPEC] * (2 * count),
        (*keeps, *recvs),
        us=0.6 * count,
    )


def spread_body(shift, meta, keep, recv, keep_out, *sends):
    rows = keep_out.shape[1]
    blocks = len(sends) + 1
    me = reversed_bits(meta[0] >> shift, blocks.bit_length() - 1)
    for t in range(blocks):
        at = pl.ds(pl.multiple_of((me ^ t) * rows, rows), rows)
        value = keep[:, at] + recv[:, at].astype(f32)
        if t:
            sends[t - 1][...] = value.astype(bf16)
        else:
            keep_out[...] = value


def spread(chain, keep, recv, shift, blocks):
    count, rows, width = keep.shape[0], keep.shape[1] // blocks, keep.shape[2]
    return chain(
        functools.partial(spread_body, shift),
        (shaped((count, rows, width), f32),) + (shaped((count, rows, width)),) * (blocks - 1),
        [VMEM_SPEC] * 2,
        (keep, recv),
        us=0.6 * count,
    )


def finish_body(meta, keep, *rest):
    total = keep[...]
    for recv in rest[:-1]:
        total = total + recv[...].astype(f32)
    rest[-1][0] = total.astype(bf16)


def finish(chain, keep, recvs):
    if keep.shape[1] % 16:
        return (keep + sum(recv.astype(f32) for recv in recvs)).astype(bf16)[None]
    return chain(finish_body, shaped((1, *keep.shape)), [VMEM_SPEC] * (1 + len(recvs)), (keep, *recvs), us=0.6)


def join_body(meta, *refs):
    at = 0
    for ref in refs[:-1]:
        refs[-1][at : at + ref.shape[0]] = ref[...]
        at += ref.shape[0]


def join(chain, parts):
    blocks, shape = sum(part.shape[0] for part in parts), parts[0].shape[1:]
    if shape[1] % 16:
        return jnp.concatenate(parts, axis=0)
    return chain(join_body, shaped((blocks, *shape)), [VMEM_SPEC] * len(parts), parts, us=0.6)


def swap_with(x, mask, size):
    return lax.ppermute(x, "outer", [(i, i ^ mask) for i in range(size)])


def prepare_body(meta, stem, out, wide):
    count, width = stem.shape[0], stem.shape[2]
    core = meta[0] & 1
    flat = stem[...].reshape(2 * count, width)
    for at in range(width // 128):
        wide[at] = flat[:, at * 128 : (at + 1) * 128].astype(f32)
    for at in range(width // 128):
        here = slice(at * 128, (at + 1) * 128)
        there = slice(width + at * 128, width + (at + 1) * 128)
        real = wide[at, pl.ds(0, count, stride=2), :]
        imag = wide[at, pl.ds(1, count, stride=2), :]
        out[core, :, here] = real.astype(bf16)
        out[core, :, there] = imag.astype(bf16)
        out[1 - core, :, here] = (-imag).astype(bf16)
        out[1 - core, :, there] = real.astype(bf16)


def prepare(chain, stem):
    count, _, width = stem.shape
    return chain(
        prepare_body,
        shaped((2, count, 2 * width)),
        [VMEM_SPEC],
        (stem,),
        [pltpu.VMEM((width // 128, 2 * count, 128), f32)],
    )


class Summed:
    def __init__(self, own, other, at):
        self.own, self.other, self.at = own, other, at
        self.parts = len(own)
        self.blocks, (self.rows, self.width) = sum(part.shape[0] for part in own), own[0].shape[2:]
        self.operands = (*own, *other)


def rows_of(refs, at):
    return jnp.concatenate([ref[:, at].reshape(-1, ref.shape[3]) for ref in refs], axis=0)


def first_body(parts, at_branch, meta, *refs):
    own, other, (right, out) = refs[:parts], refs[parts : 2 * parts], refs[2 * parts :]
    blocks, rows, columns = out.shape
    me = block_of(meta, blocks)
    mine, theirs = rows_of(own, at_branch), rows_of(other, at_branch)
    for at in range(columns // TILE):
        here = slice(at * TILE, (at + 1) * TILE)
        value = dot(mine, right[0, :, here]) + dot(theirs, right[1, :, here])
        value = value.astype(bf16).reshape(blocks, rows, TILE)
        for t in range(blocks):
            out[me ^ t, :, here] = value[t]


def first_product(chain, branch, right):
    return chain(
        functools.partial(first_body, branch.parts, branch.at),
        shaped((branch.blocks, branch.rows, 2 * branch.width)),
        [VMEM_SPEC] * (2 * branch.parts + 1),
        (*branch.operands, right),
        us=2.8,
    )


def joined_body(parts, at0, at1, meta, *refs):
    own0, other0, own1, other1 = (refs[at * parts : (at + 1) * parts] for at in range(4))
    out, right = refs[4 * parts :]
    _, blocks, rows, columns = out.shape
    width = columns // 2
    me = block_of(meta, blocks)
    core = meta[0] & 1
    t = 0
    for own_ref, other_ref in zip(own1, other1, strict=True):
        for at in range(own_ref.shape[0]):
            own, other = own_ref[at, at1], other_ref[at, at1]
            real = jnp.where(core == 0, own, other)
            imag = jnp.where(core == 0, other, own)
            right[core, me ^ t, :, :width] = real
            right[core, me ^ t, :, width:] = imag
            right[1 - core, me ^ t, :, :width] = -imag
            right[1 - core, me ^ t, :, width:] = real
            t += 1
    mine, theirs = rows_of(own0, at0), rows_of(other0, at0)
    for at in range(columns // TILE):
        here = slice(at * TILE, (at + 1) * TILE)
        there = slice((at * TILE + width) % columns, (at * TILE + width) % columns + TILE)
        first = right[0, :, :, here].reshape(blocks * rows, TILE)
        second = right[1, :, :, here].reshape(blocks * rows, TILE)
        value = dot(mine, first) + dot(theirs, second)
        turned = value if at * TILE < width else -value
        value = value.astype(bf16).reshape(blocks, rows, TILE)
        turned = turned.astype(bf16).reshape(blocks, rows, TILE)
        for t in range(blocks):
            out[0, me ^ t, :, here] = value[t]
            out[1, me ^ t, :, there] = turned[t]


def joined_right(chain, first, second):
    blocks, rows, width = first.blocks, first.rows, first.width
    return chain(
        functools.partial(joined_body, first.parts, first.at, second.at),
        shaped((2, blocks, rows, 2 * width)),
        [VMEM_SPEC] * (4 * first.parts),
        (*first.operands, *second.operands),
        [pltpu.VMEM((2, blocks, rows, 2 * width), bf16)],
        us=2.0,
    )


def last_body(parts, at_branch, meta, *refs):
    own, other = refs[:parts], refs[parts : 2 * parts]
    stem, factor, out, left, given, both, right, middle, wide, done, sems = refs[2 * parts :]
    _, blocks, rows, width = left.shape
    total = blocks * rows
    core = meta[0] & 1
    me = block_of(meta, blocks)
    copies = [pltpu.make_async_copy(stem, given, sems.at[0]), pltpu.make_async_copy(factor, both, sems.at[1])]
    for plane, refs_of in enumerate((own, other)):
        at = 0
        for ref in refs_of:
            size = ref.shape[0]
            copies.append(
                pltpu.make_async_copy(
                    ref.at[:, at_branch], left.at[plane, pl.ds(at, size)], sems.at[len(copies)]
                )
            )
            at += size
    for copy in copies:
        copy.start()
    copies[0].wait()
    value = given[...]
    right[core] = value
    right[1 - core, :, :width] = -value[:, width:]
    right[1 - core, :, width:] = value[:, :width]
    for copy in copies[2:]:
        copy.wait()
    mine = left[0].reshape(total, width)
    theirs = left[1].reshape(total, width)
    for at in range(2 * width // TILE):
        here = slice(at * TILE, (at + 1) * TILE)
        middle[:, here] = (dot(mine, right[0, :, here]) + dot(theirs, right[1, :, here])).astype(bf16)
    copies[1].wait()
    for at in range(width // TILE):
        for part in range(2):
            here = slice(part * width + at * TILE, part * width + (at + 1) * TILE)
            value = dot(middle[:, :width], both[0, :, here]) + dot(middle[:, width:], both[1, :, here])
            for sub in range(TILE // 128):
                wide[at * (TILE // 128) + sub, pl.ds(part, total, stride=2), :] = value[:, sub * 128 : (sub + 1) * 128]
    target = out.reshape(blocks, 2 * rows, width)
    writes = []
    for t in range(blocks):
        for at in range(width // 128):
            piece = wide[at, 2 * rows * t : 2 * rows * (t + 1), :]
            done[t, :, at * 128 : (at + 1) * 128] = piece.astype(bf16)
        writes.append(pltpu.make_async_copy(done.at[t], target.at[me ^ t], sems.at[len(copies) + t]))
        writes[-1].start()
    for copy in writes:
        copy.wait()


def last_product(chain, branch, stem, factor, shape):
    blocks, rows, width = branch.blocks, branch.rows, branch.width
    count = stem.shape[0]
    return chain(
        functools.partial(last_body, branch.parts, branch.at),
        shaped(shape),
        [ANY_SPEC] * (2 * branch.parts + 2),
        (*branch.operands, stem, factor),
        [
            pltpu.VMEM((2, blocks, rows, width), bf16),
            pltpu.VMEM((count, 2 * width), bf16),
            pltpu.VMEM((2, width, 2 * width), bf16),
            pltpu.VMEM((2, count, 2 * width), bf16),
            pltpu.VMEM((blocks * rows, 2 * width), bf16),
            pltpu.VMEM((width // 128, 2 * blocks * rows, 128), f32),
            pltpu.VMEM((blocks, 2 * rows, width), bf16),
            pltpu.SemaphoreType.DMA((2 + 2 * branch.parts + blocks,)),
        ],
        [ANY_SPEC],
        us=5.0,
    )


def exchange(x):
    return lax.all_to_all(x, "outer", split_axis=0, concat_axis=0, tiled=True)


class Sum:
    def __init__(self, chain, size):
        self.chain, self.size = chain, size
        self.levels = size.bit_length() - 1
        self.keeps, self.recvs = [], []

    def add(self, left, right, branch):
        keep, send = leaf_partial(self.chain, left, right, branch)
        self.keeps.append(keep)
        self.recvs.append(self.swap(send, 0))

    def swap(self, x, shift):
        return swap_with(x, 1 << shift, self.size)

    def steps(self):
        levels, chain = self.levels, self.chain
        blocks = 1 << (levels - 2)
        rows = self.keeps[0].shape[0] // (2 * blocks)
        keep, send = halve(chain, self.keeps, self.recvs, 1)
        recv = self.swap(send, 1)
        yield
        if rows % 16:
            for shift in range(2, levels):
                keep, send = halve(chain, list(keep), list(recv), shift)
                recv = self.swap(send, shift)
            total = finish(chain, keep, [recv])
            for shift in reversed(range(2, levels)):
                total = join(chain, (total, self.swap(total, shift)))
        else:
            masks = [reversed_bits(t, levels - 2) << 2 for t in range(1, blocks)]
            keep, *sends = spread(chain, keep, recv, 2, blocks)
            recvs = [swap_with(x, mask, self.size) for x, mask in zip(sends, masks, strict=True)]
            yield
            total = finish(chain, keep, recvs)
            recvs = [swap_with(total, mask, self.size) for mask in masks]
            yield
            total = join(chain, (total, *recvs))
        across = self.swap(total, 1)
        self.own, self.other = (total, across), (self.swap(total, 0), self.swap(across, 0))
        if rows % 16:
            order = block_of(chain.meta, 2 * blocks) ^ jnp.arange(2 * blocks)
            self.own, self.other = (
                (jnp.swapaxes(jnp.concatenate(x, axis=0)[order], 0, 1).reshape(1, keep.shape[0], -1, keep.shape[2]),)
                for x in (self.own, self.other)
            )
        yield

    def result(self, at):
        return Summed(self.own, self.other, at)


def on_device(size, stem_tensor, leaf_left, leaf_right, slice_bits):
    width = stem_tensor.shape[1]
    place = lax.axis_index("outer").astype(jnp.int32)
    chain = Chain(jnp.concatenate([place[None], slice_bits.astype(jnp.int32)]))
    given = exchange(stem_tensor[0])
    early, late = Sum(chain, size), Sum(chain, size)
    early.add(leaf_left, leaf_right, 0)
    late.add(leaf_left, leaf_right, 2)
    first = early.steps()
    next(first)
    late.add(leaf_left, leaf_right, 1)
    late.add(leaf_left, leaf_right, 3)
    second = late.steps()
    next(second)
    next(first)
    right = prepare(chain, given)
    next(first, None)
    next(second, None)
    next(first, None)
    next(second, None)
    state = first_product(chain, early.result(0), right).reshape(width, 2 * width)
    state = exchange(state)
    next(second, None)
    factor = joined_right(chain, late.result(1), late.result(2)).reshape(2, width, 2 * width)
    return last_product(chain, late.result(0), state, factor, stem_tensor.shape)


def solution(mesh):
    return jax.shard_map(
        functools.partial(on_device, mesh.shape["outer"]),
        mesh=mesh,
        in_specs=(
            P(("cuts", "outer"), None, None, None),
            P(None, None, "outer", None, None),
            P(None, None, "outer", None, None),
            P("cuts"),
        ),
        out_specs=P(("cuts", "outer"), None, None, None),
        check_vma=False,
    )
```

```python
import functools

import jax
import jax.numpy as jnp
from jax import lax
from jax.experimental import pallas as pl
from jax.experimental.pallas import tpu as pltpu
from jax.sharding import PartitionSpec as P

VMEM_LIMIT = 24 << 20
LEAF_LIMIT = 48 << 20
LEAF, HALVE, SPREAD, FINISH, JOIN = 0.1, 2.0, 10.0, 10.0, 10.0
PREPARE, FIRST, JOINED, LAST = 1.0, 2.8, 2.0, 5.0
TILE = 256
bf16, f32 = jnp.bfloat16, jnp.float32

SMEM_SPEC = pl.BlockSpec(memory_space=pltpu.SMEM)
VMEM_SPEC = pl.BlockSpec(memory_space=pltpu.VMEM)
ANY_SPEC = pl.BlockSpec(memory_space=pl.ANY)
HBM_SPEC = pl.BlockSpec(memory_space=pltpu.HBM)


class Calls:
    def __init__(self, meta):
        self.meta, self.last = meta, ()

    def __call__(self, body, shapes, in_specs, operands, scratch=(), out_specs=None, us=1.0, limit=VMEM_LIMIT):
        many = isinstance(shapes, (tuple, list))
        shapes = tuple(shapes) if many else (shapes,)
        after = self.last
        specs = [SMEM_SPEC] + list(in_specs) + [ANY_SPEC] * len(after)
        count = len(specs)

        def kernel(*refs):
            body(*refs[: len(in_specs) + 1], *refs[count:])

        out = pl.pallas_call(
            kernel,
            out_shape=shapes,
            in_specs=specs,
            out_specs=tuple(out_specs or [VMEM_SPEC] * len(shapes)),
            scratch_shapes=list(scratch),
            compiler_params=pltpu.CompilerParams(vmem_limit_bytes=limit),
            cost_estimate=pl.CostEstimate(flops=int(us * 1e9), bytes_accessed=1024, transcendentals=0),
        )(self.meta, *operands, *after)
        self.last = (out[0],)
        return out if many else out[0]


def shaped(shape, dtype=bf16):
    return jax.ShapeDtypeStruct(shape, dtype)


def tdot(a, b):
    return lax.dot_general(a, b, (((0,), (0,)), ((), ())), preferred_element_type=f32)


def dot(a, b):
    return jnp.dot(a, b, preferred_element_type=f32)


def reversed_bits(value, bits):
    found = 0
    for at in range(bits):
        found = found + ((value >> at) & 1) * (1 << (bits - 1 - at))
    return found


def block_of(meta, blocks):
    return reversed_bits(meta[0] >> 1, blocks.bit_length() - 1)


def leaf_body(groups, meta, left, right, *refs):
    outs, (lhs, rhs, both, sems) = refs[:-4], refs[-4:]
    depth, width = left.shape[2], left.shape[4]
    core = meta[0] & 1
    keep_at = pl.ds(pl.multiple_of(core * width, width), width)
    send_at = pl.ds(pl.multiple_of((1 - core) * width, width), width)
    branches = [branch for group in groups for branch in group]
    copies = []
    for at, branch in enumerate(branches):
        first, second = (right, left) if branch % 2 == 0 else (left, right)
        for which, (ref, buf) in enumerate(((second, rhs), (first, lhs))):
            flat = ref.reshape(ref.shape[0], ref.shape[1], 2 * depth, width)
            copies.append(
                pltpu.make_async_copy(flat.at[branch, meta[1 + branch]], buf.at[at], sems.at[at, which])
            )
            copies[-1].start()
    rows = lax.broadcasted_iota(jnp.int32, (2 * depth // 8, 8, width), 1)
    is_real = (rows & 1) == 0
    at = 0
    for group, keep, send in zip(groups, outs[0::2], outs[1::2], strict=True):
        for inside in range(len(group)):
            copies[2 * at].wait()
            wide = rhs[at].astype(f32).reshape(2 * depth // 8, 8, width)
            signed = jnp.where(is_real, wide, -wide)
            swapped = jnp.where(is_real, pltpu.roll(wide, 7, 1), pltpu.roll(wide, 1, 1))
            both[at % 2, :, keep_at] = signed.reshape(2 * depth, width).astype(bf16)
            both[at % 2, :, send_at] = swapped.reshape(2 * depth, width).astype(bf16)
            copies[2 * at + 1].wait()
            value = tdot(lhs[at], both[at % 2])
            keep[inside] = value[:, :width]
            send[inside] = value[:, width:].astype(bf16)
            at += 1


def leaf_partials(chain, left, right, groups):
    depth, width = left.shape[2], left.shape[4]
    count = sum(len(group) for group in groups)
    shapes = [shaped((len(group), width, width), dtype) for group in groups for dtype in (f32, bf16)]
    outs = chain(
        functools.partial(leaf_body, groups),
        shapes,
        [ANY_SPEC, ANY_SPEC],
        (left, right),
        [
            pltpu.VMEM((count, 2 * depth, width), bf16),
            pltpu.VMEM((count, 2 * depth, width), bf16),
            pltpu.VMEM((2, 2 * depth, 2 * width), bf16),
            pltpu.SemaphoreType.DMA((count, 2)),
        ],
        us=LEAF,
        limit=LEAF_LIMIT,
    )
    return list(zip(outs[0::2], outs[1::2], strict=True))


def half_body(shift, meta, keep, recv, keep_out, send_out):
    half = keep_out.shape[1]
    bit = (meta[0] >> shift) & 1
    mine = pl.ds(pl.multiple_of(bit * half, half), half)
    other = pl.ds(pl.multiple_of((1 - bit) * half, half), half)
    send_out[...] = (keep[:, other] + recv[:, other].astype(f32)).astype(bf16)
    keep_out[...] = keep[:, mine] + recv[:, mine].astype(f32)


def halve(chain, keep, recv, shift):
    count, rows, width = keep.shape
    half = rows // 2
    if half % 16:
        total = (keep + recv.astype(f32)).reshape(count, 2, half, width)
        bit = (chain.meta[0] >> shift) & 1
        return total[:, bit], total[:, 1 - bit].astype(bf16)
    return chain(
        functools.partial(half_body, shift),
        (shaped((count, half, width), f32), shaped((count, half, width))),
        [VMEM_SPEC] * 2,
        (keep, recv),
        us=HALVE,
    )


def spread_body(shift, meta, keep, recv, keep_out, *sends):
    rows = keep_out.shape[1]
    blocks = len(sends) + 1
    me = reversed_bits(meta[0] >> shift, blocks.bit_length() - 1)
    for t in range(blocks):
        at = pl.ds(pl.multiple_of((me ^ t) * rows, rows), rows)
        value = keep[:, at] + recv[:, at].astype(f32)
        if t:
            sends[t - 1][...] = value.astype(bf16)
        else:
            keep_out[...] = value


def spread(chain, keep, recv, shift, blocks):
    count, rows, width = keep.shape[0], keep.shape[1] // blocks, keep.shape[2]
    return chain(
        functools.partial(spread_body, shift),
        (shaped((count, rows, width), f32),) + (shaped((count, rows, width)),) * (blocks - 1),
        [VMEM_SPEC] * 2,
        (keep, recv),
        us=SPREAD,
    )


def finish_body(meta, keep, *rest):
    total = keep[...]
    for recv in rest[:-1]:
        total = total + recv[...].astype(f32)
    rest[-1][0] = total.astype(bf16)


def finish(chain, keep, recvs):
    if keep.shape[1] % 16:
        return (keep + sum(recv.astype(f32) for recv in recvs)).astype(bf16)[None]
    return chain(finish_body, shaped((1, *keep.shape)), [VMEM_SPEC] * (1 + len(recvs)), (keep, *recvs), us=FINISH)


def join_body(meta, *refs):
    at = 0
    for ref in refs[:-1]:
        refs[-1][at : at + ref.shape[0]] = ref[...]
        at += ref.shape[0]


def join(chain, parts):
    blocks, shape = sum(part.shape[0] for part in parts), parts[0].shape[1:]
    if shape[1] % 16:
        return jnp.concatenate(parts, axis=0)
    return chain(join_body, shaped((blocks, *shape)), [VMEM_SPEC] * len(parts), parts, us=JOIN)


def swap_with(x, mask, size):
    return lax.ppermute(x, "outer", [(i, i ^ mask) for i in range(size)])


def prepare_body(meta, stem, out, wide):
    count, width = stem.shape[0], stem.shape[2]
    core = meta[0] & 1
    flat = stem[...].reshape(2 * count, width)
    for at in range(width // 128):
        wide[at] = flat[:, at * 128 : (at + 1) * 128].astype(f32)
    for at in range(width // 128):
        here = slice(at * 128, (at + 1) * 128)
        there = slice(width + at * 128, width + (at + 1) * 128)
        real = wide[at, pl.ds(0, count, stride=2), :]
        imag = wide[at, pl.ds(1, count, stride=2), :]
        out[core, :, here] = real.astype(bf16)
        out[core, :, there] = imag.astype(bf16)
        out[1 - core, :, here] = (-imag).astype(bf16)
        out[1 - core, :, there] = real.astype(bf16)


def prepare(chain, stem):
    count, _, width = stem.shape
    return chain(
        prepare_body,
        shaped((2, count, 2 * width)),
        [VMEM_SPEC],
        (stem,),
        [pltpu.VMEM((width // 128, 2 * count, 128), f32)],
        us=PREPARE,
    )


class Summed:
    def __init__(self, own, other, at):
        self.own, self.other, self.at = own, other, at
        self.parts = len(own)
        self.blocks, (self.rows, self.width) = sum(part.shape[0] for part in own), own[0].shape[2:]
        self.operands = (*own, *other)


def rows_of(refs, at):
    return jnp.concatenate([ref[:, at].reshape(-1, ref.shape[3]) for ref in refs], axis=0)


def first_body(parts, at_branch, meta, *refs):
    own, other, (right, out) = refs[:parts], refs[parts : 2 * parts], refs[2 * parts :]
    blocks, rows, columns = out.shape
    me = block_of(meta, blocks)
    mine, theirs = rows_of(own, at_branch), rows_of(other, at_branch)
    for at in range(columns // TILE):
        here = slice(at * TILE, (at + 1) * TILE)
        value = dot(mine, right[0, :, here]) + dot(theirs, right[1, :, here])
        value = value.astype(bf16).reshape(blocks, rows, TILE)
        for t in range(blocks):
            out[me ^ t, :, here] = value[t]


def first_product(chain, branch, right):
    return chain(
        functools.partial(first_body, branch.parts, branch.at),
        shaped((branch.blocks, branch.rows, 2 * branch.width)),
        [VMEM_SPEC] * (2 * branch.parts + 1),
        (*branch.operands, right),
        us=FIRST,
    )


def joined_body(parts, at0, at1, at2, meta, *refs):
    own0, other0, own1, other1, own2, other2 = (refs[at * parts : (at + 1) * parts] for at in range(6))
    result, moved, right, out, sems = refs[-5:]
    copies = []
    for plane, refs_of in enumerate((own2, other2)):
        at = 0
        for ref in refs_of:
            size = ref.shape[0]
            copies.append(
                pltpu.make_async_copy(ref.at[:, at2], moved.at[plane, pl.ds(at, size)], sems.at[len(copies)])
            )
            copies[-1].start()
            at += size
    blocks, rows, columns = out.shape
    width = columns // 2
    me = block_of(meta, blocks)
    core = meta[0] & 1
    t = 0
    for own_ref, other_ref in zip(own1, other1, strict=True):
        for at in range(own_ref.shape[0]):
            own, other = own_ref[at, at1], other_ref[at, at1]
            real = jnp.where(core == 0, own, other)
            imag = jnp.where(core == 0, other, own)
            right[core, me ^ t, :, :width] = real
            right[core, me ^ t, :, width:] = imag
            right[1 - core, me ^ t, :, :width] = -imag
            right[1 - core, me ^ t, :, width:] = real
            t += 1
    mine, theirs = rows_of(own0, at0), rows_of(other0, at0)
    for at in range(columns // TILE):
        here = slice(at * TILE, (at + 1) * TILE)
        first = right[0, :, :, here].reshape(blocks * rows, TILE)
        second = right[1, :, :, here].reshape(blocks * rows, TILE)
        value = dot(mine, first) + dot(theirs, second)
        value = value.astype(bf16).reshape(blocks, rows, TILE)
        for t in range(blocks):
            out[me ^ t, :, here] = value[t]
    copies.append(pltpu.make_async_copy(out, result, sems.at[len(copies)]))
    copies[-1].start()
    for copy in copies:
        copy.wait()


def joined_right(chain, first, second, third):
    blocks, rows, width = first.blocks, first.rows, first.width
    return chain(
        functools.partial(joined_body, first.parts, first.at, second.at, third.at),
        (shaped((blocks, rows, 2 * width)), shaped((2, blocks, rows, width))),
        [VMEM_SPEC] * (4 * first.parts) + [ANY_SPEC] * (2 * first.parts),
        (*first.operands, *second.operands, *third.operands),
        [
            pltpu.VMEM((2, blocks, rows, 2 * width), bf16),
            pltpu.VMEM((blocks, rows, 2 * width), bf16),
            pltpu.SemaphoreType.DMA((1 + 2 * first.parts,)),
        ],
        [HBM_SPEC] * 2,
        us=JOINED,
    )


def last_body(meta, planes, stem, factor, out, left, given, both, right, middle, wide, done, sems):
    _, blocks, rows, width = left.shape
    total = blocks * rows
    core = meta[0] & 1
    me = block_of(meta, blocks)
    copies = [
        pltpu.make_async_copy(source, target, sems.at[at])
        for at, (source, target) in enumerate(((stem, given), (factor, both.at[0]), (planes, left)))
    ]
    for copy in copies:
        copy.start()
    copies[0].wait()
    value = given[...]
    right[core] = value
    right[1 - core, :, :width] = -value[:, width:]
    right[1 - core, :, width:] = value[:, :width]
    for copy in copies[2:]:
        copy.wait()
    mine = left[0].reshape(total, width)
    theirs = left[1].reshape(total, width)
    for at in range(2 * width // TILE):
        here = slice(at * TILE, (at + 1) * TILE)
        middle[:, here] = (dot(mine, right[0, :, here]) + dot(theirs, right[1, :, here])).astype(bf16)
    copies[1].wait()
    value = both[0]
    both[1, :, :width] = -value[:, width:]
    both[1, :, width:] = value[:, :width]
    for at in range(width // TILE):
        for part in range(2):
            here = slice(part * width + at * TILE, part * width + (at + 1) * TILE)
            value = dot(middle[:, :width], both[0, :, here]) + dot(middle[:, width:], both[1, :, here])
            for sub in range(TILE // 128):
                wide[at * (TILE // 128) + sub, pl.ds(part, total, stride=2), :] = value[:, sub * 128 : (sub + 1) * 128]
    target = out.reshape(blocks, 2 * rows, width)
    writes = []
    for t in range(blocks):
        for at in range(width // 128):
            piece = wide[at, 2 * rows * t : 2 * rows * (t + 1), :]
            done[t, :, at * 128 : (at + 1) * 128] = piece.astype(bf16)
        writes.append(pltpu.make_async_copy(done.at[t], target.at[me ^ t], sems.at[len(copies) + t]))
        writes[-1].start()
    for copy in writes:
        copy.wait()


def last_product(chain, planes, stem, factor, shape):
    _, blocks, rows, width = planes.shape
    count = stem.shape[0]
    return chain(
        last_body,
        shaped(shape),
        [HBM_SPEC, ANY_SPEC, HBM_SPEC],
        (planes, stem, factor),
        [
            pltpu.VMEM((2, blocks, rows, width), bf16),
            pltpu.VMEM((count, 2 * width), bf16),
            pltpu.VMEM((2, width, 2 * width), bf16),
            pltpu.VMEM((2, count, 2 * width), bf16),
            pltpu.VMEM((blocks * rows, 2 * width), bf16),
            pltpu.VMEM((width // 128, 2 * blocks * rows, 128), f32),
            pltpu.VMEM((blocks, 2 * rows, width), bf16),
            pltpu.SemaphoreType.DMA((3 + blocks,)),
        ],
        [ANY_SPEC],
        us=LAST,
    )


def exchange(x):
    return lax.all_to_all(x, "outer", split_axis=0, concat_axis=0, tiled=True)


class Sum:
    def __init__(self, chain, size, keep, send):
        self.chain, self.size = chain, size
        self.levels = size.bit_length() - 1
        self.keep, self.recv = keep, self.swap(send, 0)

    def swap(self, x, shift):
        return swap_with(x, 1 << shift, self.size)

    def steps(self):
        levels, chain = self.levels, self.chain
        blocks = 1 << (levels - 2)
        rows = self.keep.shape[1] // (2 * blocks)
        keep, send = halve(chain, self.keep, self.recv, 1)
        recv = self.swap(send, 1)
        yield
        if rows % 16:
            for shift in range(2, levels):
                keep, send = halve(chain, keep, recv, shift)
                recv = self.swap(send, shift)
            total = finish(chain, keep, [recv])
            for shift in reversed(range(2, levels)):
                total = join(chain, (total, self.swap(total, shift)))
        else:
            masks = [reversed_bits(t, levels - 2) << 2 for t in range(1, blocks)]
            keep, *sends = spread(chain, keep, recv, 2, blocks)
            recvs = [swap_with(x, mask, self.size) for x, mask in zip(sends, masks, strict=True)]
            yield
            total = finish(chain, keep, recvs)
            recvs = [swap_with(total, mask, self.size) for mask in masks]
            yield
            total = join(chain, (total, *recvs))
        across = self.swap(total, 1)
        self.own, self.other = (total, across), (self.swap(total, 0), self.swap(across, 0))
        if rows % 16:
            order = block_of(chain.meta, 2 * blocks) ^ jnp.arange(2 * blocks)
            self.own, self.other = (
                (jnp.swapaxes(jnp.concatenate(x, axis=0)[order], 0, 1).reshape(1, keep.shape[0], -1, keep.shape[2]),)
                for x in (self.own, self.other)
            )
        yield

    def result(self, at):
        return Summed(self.own, self.other, at)


def on_device(size, stem_tensor, leaf_left, leaf_right, slice_bits):
    width = stem_tensor.shape[1]
    place = lax.axis_index("outer").astype(jnp.int32)
    chain = Calls(jnp.concatenate([place[None], slice_bits.astype(jnp.int32)]))
    given = exchange(stem_tensor[0])
    groups = (0,), (2,), (1, 3)
    sums = [Sum(chain, size, *parts) for parts in leaf_partials(chain, leaf_left, leaf_right, groups)]
    p0, p1, q = (total.steps() for total in sums)
    next(p0, None)
    next(p1, None)
    next(q, None)
    right = prepare(chain, given)
    next(p0, None)
    next(p1, None)
    next(p0, None)
    next(p1, None)
    next(q, None)
    next(p0, None)
    next(p1, None)
    next(q, None)
    state = first_product(chain, sums[0].result(0), right).reshape(width, 2 * width)
    state = exchange(state)
    next(q, None)
    factor, planes = joined_right(chain, sums[2].result(0), sums[2].result(1), sums[1].result(0))
    return last_product(chain, planes, state, factor.reshape(width, 2 * width), stem_tensor.shape)


def solution(mesh):
    return jax.shard_map(
        functools.partial(on_device, mesh.shape["outer"]),
        mesh=mesh,
        in_specs=(
            P(("cuts", "outer"), None, None, None),
            P(None, None, "outer", None, None),
            P(None, None, "outer", None, None),
            P("cuts"),
        ),
        out_specs=P(("cuts", "outer"), None, None, None),
        check_vma=False,
    )
```

```python
import functools

import jax
import jax.numpy as jnp
from jax import lax
from jax.experimental import pallas as pl
from jax.experimental.pallas import tpu as pltpu
from jax.sharding import PartitionSpec as P

VMEM_LIMIT = 24 << 20
LEAF_LIMIT = 48 << 20
DIRECT = True, True, True
LEAVES = 0.1, 10.0
STEPS = (1.0, 20.0, 20.0, 10.0), (2.0, 3.0, 20.0, 20.0), (3.0, 5.0, 10.0, 20.0)
PREPARE, FIRST, JOINED, LAST = 5.0, 0.1, 2.0, 5.0
RIGHT = 2.0
TILE = 256
bf16, f32 = jnp.bfloat16, jnp.float32

SMEM_SPEC = pl.BlockSpec(memory_space=pltpu.SMEM)
VMEM_SPEC = pl.BlockSpec(memory_space=pltpu.VMEM)
ANY_SPEC = pl.BlockSpec(memory_space=pl.ANY)
HBM_SPEC = pl.BlockSpec(memory_space=pltpu.HBM)


class Calls:
    def __init__(self, meta):
        self.meta, self.last = meta, ()

    def __call__(self, body, shapes, in_specs, operands, scratch=(), out_specs=None, us=1.0, limit=VMEM_LIMIT):
        many = isinstance(shapes, (tuple, list))
        shapes = tuple(shapes) if many else (shapes,)
        after = self.last
        specs = [SMEM_SPEC] + list(in_specs) + [ANY_SPEC] * len(after)
        count = len(specs)

        def kernel(*refs):
            body(*refs[: len(in_specs) + 1], *refs[count:])

        out = pl.pallas_call(
            kernel,
            out_shape=shapes,
            in_specs=specs,
            out_specs=tuple(out_specs or [VMEM_SPEC] * len(shapes)),
            scratch_shapes=list(scratch),
            compiler_params=pltpu.CompilerParams(vmem_limit_bytes=limit),
            cost_estimate=pl.CostEstimate(flops=int(us * 1e9), bytes_accessed=1024, transcendentals=0),
        )(self.meta, *operands, *after)
        self.last = (out[0],)
        return out if many else out[0]


def shaped(shape, dtype=bf16):
    return jax.ShapeDtypeStruct(shape, dtype)


def tdot(a, b):
    return lax.dot_general(a, b, (((0,), (0,)), ((), ())), preferred_element_type=f32)


def dot(a, b):
    return jnp.dot(a, b, preferred_element_type=f32)


def reversed_bits(value, bits):
    found = 0
    for at in range(bits):
        found = found + ((value >> at) & 1) * (1 << (bits - 1 - at))
    return found


def block_of(meta, blocks):
    return reversed_bits(meta[0] >> 1, blocks.bit_length() - 1)


def leaf_body(groups, meta, left, right, *refs):
    outs, (lhs, rhs, both, sems) = refs[:-4], refs[-4:]
    depth, width = left.shape[2], left.shape[4]
    core = meta[0] & 1
    keep_at = pl.ds(pl.multiple_of(core * width, width), width)
    send_at = pl.ds(pl.multiple_of((1 - core) * width, width), width)
    branches = [branch for group in groups for branch in group]
    copies = []
    for at, branch in enumerate(branches):
        first, second = (right, left) if branch % 2 == 0 else (left, right)
        for which, (ref, buf) in enumerate(((second, rhs), (first, lhs))):
            flat = ref.reshape(ref.shape[0], ref.shape[1], 2 * depth, width)
            copies.append(
                pltpu.make_async_copy(flat.at[branch, meta[1 + branch]], buf.at[at], sems.at[at, which])
            )
            copies[-1].start()
    rows = lax.broadcasted_iota(jnp.int32, (2 * depth // 8, 8, width), 1)
    is_real = (rows & 1) == 0
    at = 0
    for group, keep, send in zip(groups, outs[0::2], outs[1::2], strict=True):
        for inside in range(len(group)):
            copies[2 * at].wait()
            wide = rhs[at].astype(f32).reshape(2 * depth // 8, 8, width)
            signed = jnp.where(is_real, wide, -wide)
            swapped = jnp.where(is_real, pltpu.roll(wide, 7, 1), pltpu.roll(wide, 1, 1))
            both[at % 2, :, keep_at] = signed.reshape(2 * depth, width).astype(bf16)
            both[at % 2, :, send_at] = swapped.reshape(2 * depth, width).astype(bf16)
            copies[2 * at + 1].wait()
            value = tdot(lhs[at], both[at % 2])
            keep[inside] = value[:, :width]
            send[inside] = value[:, width:].astype(bf16)
            at += 1


def leaf_partials(chain, left, right, groups, us):
    depth, width = left.shape[2], left.shape[4]
    count = sum(len(group) for group in groups)
    shapes = [shaped((len(group), width, width), dtype) for group in groups for dtype in (f32, bf16)]
    outs = chain(
        functools.partial(leaf_body, groups),
        shapes,
        [ANY_SPEC, ANY_SPEC],
        (left, right),
        [
            pltpu.VMEM((count, 2 * depth, width), bf16),
            pltpu.VMEM((count, 2 * depth, width), bf16),
            pltpu.VMEM((2, 2 * depth, 2 * width), bf16),
            pltpu.SemaphoreType.DMA((count, 2)),
        ],
        us=us,
        limit=LEAF_LIMIT,
    )
    return list(zip(outs[0::2], outs[1::2], strict=True))


def half_body(shift, meta, keep, recv, keep_out, send_out):
    half = keep_out.shape[1]
    bit = (meta[0] >> shift) & 1
    mine = pl.ds(pl.multiple_of(bit * half, half), half)
    other = pl.ds(pl.multiple_of((1 - bit) * half, half), half)
    send_out[...] = (keep[:, other] + recv[:, other].astype(f32)).astype(bf16)
    keep_out[...] = keep[:, mine] + recv[:, mine].astype(f32)


def halve(chain, keep, recv, shift, us):
    count, rows, width = keep.shape
    half = rows // 2
    if half % 16:
        total = (keep + recv.astype(f32)).reshape(count, 2, half, width)
        bit = (chain.meta[0] >> shift) & 1
        return total[:, bit], total[:, 1 - bit].astype(bf16)
    return chain(
        functools.partial(half_body, shift),
        (shaped((count, half, width), f32), shaped((count, half, width))),
        [VMEM_SPEC] * 2,
        (keep, recv),
        us=us,
    )


def spread_body(shift, meta, keep, recv, keep_out, *sends):
    rows = keep_out.shape[1]
    blocks = len(sends) + 1
    me = reversed_bits(meta[0] >> shift, blocks.bit_length() - 1)
    for t in range(blocks):
        at = pl.ds(pl.multiple_of((me ^ t) * rows, rows), rows)
        value = keep[:, at] + recv[:, at].astype(f32)
        if t:
            sends[t - 1][...] = value.astype(bf16)
        else:
            keep_out[...] = value


def spread(chain, keep, recv, shift, blocks, us):
    count, rows, width = keep.shape[0], keep.shape[1] // blocks, keep.shape[2]
    return chain(
        functools.partial(spread_body, shift),
        (shaped((count, rows, width), f32),) + (shaped((count, rows, width)),) * (blocks - 1),
        [VMEM_SPEC] * 2,
        (keep, recv),
        us=us,
    )


def finish_body(meta, keep, *rest):
    total = keep[...]
    for recv in rest[:-1]:
        total = total + recv[...].astype(f32)
    rest[-1][0] = total.astype(bf16)


def finish(chain, keep, recvs, us):
    if keep.shape[1] % 16:
        return (keep + sum(recv.astype(f32) for recv in recvs)).astype(bf16)[None]
    return chain(finish_body, shaped((1, *keep.shape)), [VMEM_SPEC] * (1 + len(recvs)), (keep, *recvs), us=us)


def join_body(meta, *refs):
    at = 0
    for ref in refs[:-1]:
        refs[-1][at : at + ref.shape[0]] = ref[...]
        at += ref.shape[0]


def join(chain, parts, us):
    blocks, shape = sum(part.shape[0] for part in parts), parts[0].shape[1:]
    if shape[1] % 16:
        return jnp.concatenate(parts, axis=0)
    return chain(join_body, shaped((blocks, *shape)), [VMEM_SPEC] * len(parts), parts, us=us)


def swap_with(x, mask, size):
    return lax.ppermute(x, "outer", [(i, i ^ mask) for i in range(size)])


def prepare_body(meta, stem, out, wide):
    count, width = stem.shape[0], stem.shape[2]
    core = meta[0] & 1
    flat = stem[...].reshape(2 * count, width)
    for at in range(width // 128):
        wide[at] = flat[:, at * 128 : (at + 1) * 128].astype(f32)
    for at in range(width // 128):
        here = slice(at * 128, (at + 1) * 128)
        there = slice(width + at * 128, width + (at + 1) * 128)
        real = wide[at, pl.ds(0, count, stride=2), :]
        imag = wide[at, pl.ds(1, count, stride=2), :]
        out[core, :, here] = real.astype(bf16)
        out[core, :, there] = imag.astype(bf16)
        out[1 - core, :, here] = (-imag).astype(bf16)
        out[1 - core, :, there] = real.astype(bf16)


def prepare(chain, stem):
    count, _, width = stem.shape
    return chain(
        prepare_body,
        shaped((2, count, 2 * width)),
        [VMEM_SPEC],
        (stem,),
        [pltpu.VMEM((width // 128, 2 * count, 128), f32)],
        us=PREPARE,
    )


class Summed:
    def __init__(self, own, other, at):
        self.own, self.other, self.at = own, other, at
        self.parts = len(own)
        self.blocks, (self.rows, self.width) = sum(part.shape[0] for part in own), own[0].shape[2:]
        self.operands = (*own, *other)


def rows_of(refs, at):
    return jnp.concatenate([ref[:, at].reshape(-1, ref.shape[3]) for ref in refs], axis=0)


def first_body(parts, at_branch, meta, *refs):
    own, other, (right, out) = refs[:parts], refs[parts : 2 * parts], refs[2 * parts :]
    blocks, rows, columns = out.shape
    me = block_of(meta, blocks)
    left = jnp.concatenate([rows_of(own, at_branch), rows_of(other, at_branch)], axis=1)
    for at in range(columns // TILE):
        here = slice(at * TILE, (at + 1) * TILE)
        value = dot(left, right[:, :, here].reshape(columns, TILE))
        value = value.astype(bf16).reshape(blocks, rows, TILE)
        for t in range(blocks):
            out[me ^ t, :, here] = value[t]


def first_product(chain, branch, right):
    return chain(
        functools.partial(first_body, branch.parts, branch.at),
        shaped((branch.blocks, branch.rows, 2 * branch.width)),
        [VMEM_SPEC] * (2 * branch.parts + 1),
        (*branch.operands, right),
        us=FIRST,
    )


def joined_body(parts, at0, at1, meta, *refs):
    own0, other0, own1, other1 = (refs[at * parts : (at + 1) * parts] for at in range(4))
    out, right = refs[4 * parts :]
    blocks, rows, columns = out.shape
    width = columns // 2
    me = block_of(meta, blocks)
    core = meta[0] & 1
    t = 0
    for own_ref, other_ref in zip(own1, other1, strict=True):
        for at in range(own_ref.shape[0]):
            own, other = own_ref[at, at1], other_ref[at, at1]
            real = jnp.where(core == 0, own, other)
            imag = jnp.where(core == 0, other, own)
            right[core, me ^ t, :, :width] = real
            right[core, me ^ t, :, width:] = imag
            right[1 - core, me ^ t, :, :width] = -imag
            right[1 - core, me ^ t, :, width:] = real
            t += 1
    left = jnp.concatenate([rows_of(own0, at0), rows_of(other0, at0)], axis=1)
    for at in range(columns // TILE):
        here = slice(at * TILE, (at + 1) * TILE)
        value = dot(left, right[:, :, :, here].reshape(columns, TILE))
        value = value.astype(bf16).reshape(blocks, rows, TILE)
        for t in range(blocks):
            out[me ^ t, :, here] = value[t]


def joined_right(chain, first, second):
    blocks, rows, width = first.blocks, first.rows, first.width
    return chain(
        functools.partial(joined_body, first.parts, first.at, second.at),
        shaped((blocks, rows, 2 * width)),
        [VMEM_SPEC] * (4 * first.parts),
        (*first.operands, *second.operands),
        [pltpu.VMEM((2, blocks, rows, 2 * width), bf16)],
        us=JOINED,
    )


def right_body(meta, stem, factor, out, both):
    count, columns = stem.shape
    width = columns // 2
    core = meta[0] & 1
    value = factor[...]
    both[:width] = value
    both[width:, :width] = -value[:, width:]
    both[width:, width:] = value[:, :width]
    left = stem[...]
    for at in range(columns // TILE):
        here = slice(at * TILE, (at + 1) * TILE)
        there = slice((at * TILE + width) % columns, (at * TILE + width) % columns + TILE)
        value = dot(left, both[:, here])
        turned = value if at * TILE < width else -value
        out[core, :, here] = value.astype(bf16)
        out[1 - core, :, there] = turned.astype(bf16)


def right_product(chain, stem, factor):
    count, columns = stem.shape
    return chain(
        right_body,
        shaped((2, count, columns)),
        [VMEM_SPEC] * 2,
        (stem, factor),
        [pltpu.VMEM((columns, columns), bf16)],
        us=RIGHT,
    )


def last_body(parts, at_branch, meta, *refs):
    own, other = refs[:parts], refs[parts : 2 * parts]
    right, out, wide, done, sems = refs[2 * parts :]
    blocks, rows, width = done.shape[0], done.shape[1] // 2, done.shape[2]
    total = blocks * rows
    me = block_of(meta, blocks)
    left = jnp.concatenate([rows_of(own, at_branch), rows_of(other, at_branch)], axis=1)
    target = out.reshape(blocks, 2 * rows, width)
    for at in range(width // TILE):
        for part in range(2):
            here = slice(part * width + at * TILE, part * width + (at + 1) * TILE)
            value = dot(left, right[:, :, here].reshape(2 * right.shape[1], TILE))
            for sub in range(TILE // 128):
                wide[at * (TILE // 128) + sub, pl.ds(part, total, stride=2), :] = value[:, sub * 128 : (sub + 1) * 128]
    writes = []
    for t in range(blocks):
        for at in range(width // 128):
            piece = wide[at, 2 * rows * t : 2 * rows * (t + 1), :]
            done[t, :, at * 128 : (at + 1) * 128] = piece.astype(bf16)
        writes.append(pltpu.make_async_copy(done.at[t], target.at[me ^ t], sems.at[t]))
        writes[-1].start()
    for copy in writes:
        copy.wait()


def last_product(chain, branch, right, shape):
    blocks, rows, width = branch.blocks, branch.rows, branch.width
    return chain(
        functools.partial(last_body, branch.parts, branch.at),
        shaped(shape),
        [VMEM_SPEC] * (2 * branch.parts + 1),
        (*branch.operands, right),
        [
            pltpu.VMEM((width // 128, 2 * blocks * rows, 128), f32),
            pltpu.VMEM((blocks, 2 * rows, width), bf16),
            pltpu.SemaphoreType.DMA((blocks,)),
        ],
        [ANY_SPEC],
        us=LAST,
    )


def exchange(x):
    return lax.all_to_all(x, "outer", split_axis=0, concat_axis=0, tiled=True)


class Sum:
    def __init__(self, chain, size, times, direct, keep, send):
        self.chain, self.size, self.times, self.direct = chain, size, times, direct
        self.levels = size.bit_length() - 1
        self.keep, self.recv = keep, self.swap(send, 0)

    def swap(self, x, shift):
        return swap_with(x, 1 << shift, self.size)

    def steps(self):
        levels, chain = self.levels, self.chain
        halve_us, spread_us, finish_us, join_us = self.times
        blocks = 1 << (levels - 2)
        rows = self.keep.shape[1] // (2 * blocks)
        keep, send = halve(chain, self.keep, self.recv, 1, halve_us)
        recv = self.swap(send, 1)
        yield
        if rows % 16 or not self.direct:
            for shift in range(2, levels):
                keep, send = halve(chain, keep, recv, shift, spread_us)
                recv = self.swap(send, shift)
                yield
            total = finish(chain, keep, [recv], finish_us)
            for shift in reversed(range(2, levels)):
                recv = self.swap(total, shift)
                yield
                total = join(chain, (total, recv), join_us)
        else:
            masks = [reversed_bits(t, levels - 2) << 2 for t in range(1, blocks)]
            keep, *sends = spread(chain, keep, recv, 2, blocks, spread_us)
            recvs = [swap_with(x, mask, self.size) for x, mask in zip(sends, masks, strict=True)]
            yield
            total = finish(chain, keep, recvs, finish_us)
            recvs = [swap_with(total, mask, self.size) for mask in masks]
            yield
            total = join(chain, (total, *recvs), join_us)
        across = self.swap(total, 1)
        self.own, self.other = (total, across), (self.swap(total, 0), self.swap(across, 0))
        if rows % 16:
            order = block_of(chain.meta, 2 * blocks) ^ jnp.arange(2 * blocks)
            self.own, self.other = (
                (jnp.swapaxes(jnp.concatenate(x, axis=0)[order], 0, 1).reshape(1, keep.shape[0], -1, keep.shape[2]),)
                for x in (self.own, self.other)
            )
        yield

    def result(self, at):
        return Summed(self.own, self.other, at)


def on_device(size, stem_tensor, leaf_left, leaf_right, slice_bits):
    width = stem_tensor.shape[1]
    place = lax.axis_index("outer").astype(jnp.int32)
    chain = Calls(jnp.concatenate([place[None], slice_bits.astype(jnp.int32)]))
    given = exchange(stem_tensor[0])
    early, late = ((0,),), ((1, 3), (2,))
    sums = [
        Sum(chain, size, times, direct, *parts)
        for times, direct, parts in zip(STEPS, DIRECT, leaf_partials(chain, leaf_left, leaf_right, early, LEAVES[0]))
    ]
    a = sums[0].steps()
    next(a, None)
    sums += [
        Sum(chain, size, times, direct, *parts)
        for times, direct, parts in zip(STEPS[1:], DIRECT[1:], leaf_partials(chain, leaf_left, leaf_right, late, LEAVES[1]))
    ]
    b, c = (total.steps() for total in sums[1:])
    next(a, None)
    next(b, None)
    right = prepare(chain, given)
    next(a, None)
    next(b, None)
    next(c, None)
    next(a, None)
    next(b, None)
    next(c, None)
    next(c, None)
    for _ in a:
        pass
    state = first_product(chain, sums[0].result(0), right).reshape(width, 2 * width)
    state = exchange(state)
    next(b, None)
    next(c, None)
    for steps in (b, c):
        for _ in steps:
            pass
    factor = joined_right(chain, sums[1].result(0), sums[1].result(1)).reshape(width, 2 * width)
    right = right_product(chain, state, factor)
    return last_product(chain, sums[2].result(0), right, stem_tensor.shape)


def solution(mesh):
    return jax.shard_map(
        functools.partial(on_device, mesh.shape["outer"]),
        mesh=mesh,
        in_specs=(
            P(("cuts", "outer"), None, None, None),
            P(None, None, "outer", None, None),
            P(None, None, "outer", None, None),
            P("cuts"),
        ),
        out_specs=P(("cuts", "outer"), None, None, None),
        check_vma=False,
    )
```

```python
import functools

import jax
import jax.numpy as jnp
from jax import lax
from jax.experimental import pallas as pl
from jax.experimental.pallas import tpu as pltpu
from jax.sharding import PartitionSpec as P

VMEM_LIMIT = 24 << 20
LEAF_LIMIT = 48 << 20
DIRECT = True, True, True
LEAVES = 0.1, 10.0
STEPS = (0.1, 20.0, 3.0, 10.0), (0.5, 20.0, 20.0, 20.0), (0.5, 5.0, 10.0, 20.0)
PREPARE, FIRST, JOINED, LAST = 0.1, 1.0, 2.0, 1.0
RIGHT = 2.0
TILE = 256
bf16, f32 = jnp.bfloat16, jnp.float32

SMEM_SPEC = pl.BlockSpec(memory_space=pltpu.SMEM)
VMEM_SPEC = pl.BlockSpec(memory_space=pltpu.VMEM)
ANY_SPEC = pl.BlockSpec(memory_space=pl.ANY)
HBM_SPEC = pl.BlockSpec(memory_space=pltpu.HBM)


class Calls:
    def __init__(self, meta):
        self.meta, self.last = meta, ()

    def __call__(self, body, shapes, in_specs, operands, scratch=(), out_specs=None, us=1.0, limit=VMEM_LIMIT):
        many = isinstance(shapes, (tuple, list))
        shapes = tuple(shapes) if many else (shapes,)
        after = self.last
        specs = [SMEM_SPEC] + list(in_specs) + [ANY_SPEC] * len(after)
        count = len(specs)

        def kernel(*refs):
            body(*refs[: len(in_specs) + 1], *refs[count:])

        out = pl.pallas_call(
            kernel,
            out_shape=shapes,
            in_specs=specs,
            out_specs=tuple(out_specs or [VMEM_SPEC] * len(shapes)),
            scratch_shapes=list(scratch),
            compiler_params=pltpu.CompilerParams(vmem_limit_bytes=limit),
            cost_estimate=pl.CostEstimate(flops=int(us * 1e9), bytes_accessed=1024, transcendentals=0),
        )(self.meta, *operands, *after)
        self.last = (out[0],)
        return out if many else out[0]


def shaped(shape, dtype=bf16):
    return jax.ShapeDtypeStruct(shape, dtype)


def tdot(a, b):
    return lax.dot_general(a, b, (((0,), (0,)), ((), ())), preferred_element_type=f32)


def dot(a, b):
    return jnp.dot(a, b, preferred_element_type=f32)


def reversed_bits(value, bits):
    found = 0
    for at in range(bits):
        found = found + ((value >> at) & 1) * (1 << (bits - 1 - at))
    return found


def block_of(meta, blocks):
    return reversed_bits(meta[0] >> 1, blocks.bit_length() - 1)


def leaf_body(groups, meta, left, right, *refs):
    outs, (lhs, rhs, both, sems) = refs[:-4], refs[-4:]
    depth, width = left.shape[2], left.shape[4]
    core = meta[0] & 1
    keep_at = pl.ds(pl.multiple_of(core * width, width), width)
    send_at = pl.ds(pl.multiple_of((1 - core) * width, width), width)
    branches = [branch for group in groups for branch in group]
    copies = []
    for at, branch in enumerate(branches):
        first, second = (right, left) if branch % 2 == 0 else (left, right)
        for which, (ref, buf) in enumerate(((second, rhs), (first, lhs))):
            flat = ref.reshape(ref.shape[0], ref.shape[1], 2 * depth, width)
            copies.append(
                pltpu.make_async_copy(flat.at[branch, meta[1 + branch]], buf.at[at], sems.at[at, which])
            )
            copies[-1].start()
    rows = lax.broadcasted_iota(jnp.int32, (2 * depth // 8, 8, width), 1)
    is_real = (rows & 1) == 0
    at = 0
    for group, keep, send in zip(groups, outs[0::2], outs[1::2], strict=True):
        for inside in range(len(group)):
            copies[2 * at].wait()
            wide = rhs[at].astype(f32).reshape(2 * depth // 8, 8, width)
            signed = jnp.where(is_real, wide, -wide)
            swapped = jnp.where(is_real, pltpu.roll(wide, 7, 1), pltpu.roll(wide, 1, 1))
            both[at % 2, :, keep_at] = signed.reshape(2 * depth, width).astype(bf16)
            both[at % 2, :, send_at] = swapped.reshape(2 * depth, width).astype(bf16)
            copies[2 * at + 1].wait()
            value = tdot(lhs[at], both[at % 2])
            keep[inside] = value[:, :width]
            send[inside] = value[:, width:].astype(bf16)
            at += 1


def leaf_partials(chain, left, right, groups, us):
    depth, width = left.shape[2], left.shape[4]
    count = sum(len(group) for group in groups)
    shapes = [shaped((len(group), width, width), dtype) for group in groups for dtype in (f32, bf16)]
    outs = chain(
        functools.partial(leaf_body, groups),
        shapes,
        [ANY_SPEC, ANY_SPEC],
        (left, right),
        [
            pltpu.VMEM((count, 2 * depth, width), bf16),
            pltpu.VMEM((count, 2 * depth, width), bf16),
            pltpu.VMEM((2, 2 * depth, 2 * width), bf16),
            pltpu.SemaphoreType.DMA((count, 2)),
        ],
        us=us,
        limit=LEAF_LIMIT,
    )
    return list(zip(outs[0::2], outs[1::2], strict=True))


def half_body(shift, meta, keep, recv, keep_out, send_out):
    half = keep_out.shape[1]
    bit = (meta[0] >> shift) & 1
    mine = pl.ds(pl.multiple_of(bit * half, half), half)
    other = pl.ds(pl.multiple_of((1 - bit) * half, half), half)
    send_out[...] = (keep[:, other] + recv[:, other].astype(f32)).astype(bf16)
    keep_out[...] = keep[:, mine] + recv[:, mine].astype(f32)


def halve(chain, keep, recv, shift, us):
    count, rows, width = keep.shape
    half = rows // 2
    if half % 16:
        total = (keep + recv.astype(f32)).reshape(count, 2, half, width)
        bit = (chain.meta[0] >> shift) & 1
        return total[:, bit], total[:, 1 - bit].astype(bf16)
    return chain(
        functools.partial(half_body, shift),
        (shaped((count, half, width), f32), shaped((count, half, width))),
        [VMEM_SPEC] * 2,
        (keep, recv),
        us=us,
    )


def spread_body(shift, meta, keep, recv, keep_out, *sends):
    rows = keep_out.shape[1]
    blocks = len(sends) + 1
    me = reversed_bits(meta[0] >> shift, blocks.bit_length() - 1)
    for t in range(blocks):
        at = pl.ds(pl.multiple_of((me ^ t) * rows, rows), rows)
        value = keep[:, at] + recv[:, at].astype(f32)
        if t:
            sends[t - 1][...] = value.astype(bf16)
        else:
            keep_out[...] = value


def spread(chain, keep, recv, shift, blocks, us):
    count, rows, width = keep.shape[0], keep.shape[1] // blocks, keep.shape[2]
    return chain(
        functools.partial(spread_body, shift),
        (shaped((count, rows, width), f32),) + (shaped((count, rows, width)),) * (blocks - 1),
        [VMEM_SPEC] * 2,
        (keep, recv),
        us=us,
    )


def finish_body(meta, keep, *rest):
    total = keep[...]
    for recv in rest[:-1]:
        total = total + recv[...].astype(f32)
    rest[-1][0] = total.astype(bf16)


def finish(chain, keep, recvs, us):
    if keep.shape[1] % 16:
        return (keep + sum(recv.astype(f32) for recv in recvs)).astype(bf16)[None]
    return chain(finish_body, shaped((1, *keep.shape)), [VMEM_SPEC] * (1 + len(recvs)), (keep, *recvs), us=us)


def join_body(meta, *refs):
    at = 0
    for ref in refs[:-1]:
        refs[-1][at : at + ref.shape[0]] = ref[...]
        at += ref.shape[0]


def join(chain, parts, us):
    blocks, shape = sum(part.shape[0] for part in parts), parts[0].shape[1:]
    if shape[1] % 16:
        return jnp.concatenate(parts, axis=0)
    return chain(join_body, shaped((blocks, *shape)), [VMEM_SPEC] * len(parts), parts, us=us)


def swap_with(x, mask, size):
    return lax.ppermute(x, "outer", [(i, i ^ mask) for i in range(size)])


def prepare_body(meta, stem, out, wide):
    count, width = stem.shape[0], stem.shape[2]
    core = meta[0] & 1
    flat = stem[...].reshape(2 * count, width)
    for at in range(width // 128):
        wide[at] = flat[:, at * 128 : (at + 1) * 128].astype(f32)
    for at in range(width // 128):
        here = slice(at * 128, (at + 1) * 128)
        there = slice(width + at * 128, width + (at + 1) * 128)
        real = wide[at, pl.ds(0, count, stride=2), :]
        imag = wide[at, pl.ds(1, count, stride=2), :]
        out[core, :, here] = real.astype(bf16)
        out[core, :, there] = imag.astype(bf16)
        out[1 - core, :, here] = (-imag).astype(bf16)
        out[1 - core, :, there] = real.astype(bf16)


def prepare(chain, stem):
    count, _, width = stem.shape
    return chain(
        prepare_body,
        shaped((2, count, 2 * width)),
        [VMEM_SPEC],
        (stem,),
        [pltpu.VMEM((width // 128, 2 * count, 128), f32)],
        us=PREPARE,
    )


class Summed:
    def __init__(self, own, other, at):
        self.own, self.other, self.at = own, other, at
        self.parts = len(own)
        self.blocks, (self.rows, self.width) = sum(part.shape[0] for part in own), own[0].shape[2:]
        self.operands = (*own, *other)


def rows_of(refs, at):
    return jnp.concatenate([ref[:, at].reshape(-1, ref.shape[3]) for ref in refs], axis=0)


def first_body(parts, at_branch, meta, *refs):
    own, other, (right, out) = refs[:parts], refs[parts : 2 * parts], refs[2 * parts :]
    blocks, rows, columns = out.shape
    me = block_of(meta, blocks)
    left = jnp.concatenate([rows_of(own, at_branch), rows_of(other, at_branch)], axis=1)
    for at in range(columns // TILE):
        here = slice(at * TILE, (at + 1) * TILE)
        value = dot(left, right[:, :, here].reshape(columns, TILE))
        value = value.astype(bf16).reshape(blocks, rows, TILE)
        for t in range(blocks):
            out[me ^ t, :, here] = value[t]


def first_product(chain, branch, right):
    return chain(
        functools.partial(first_body, branch.parts, branch.at),
        shaped((branch.blocks, branch.rows, 2 * branch.width)),
        [VMEM_SPEC] * (2 * branch.parts + 1),
        (*branch.operands, right),
        us=FIRST,
    )


def joined_body(parts, at0, at1, meta, *refs):
    own0, other0, own1, other1 = (refs[at * parts : (at + 1) * parts] for at in range(4))
    out, right = refs[4 * parts :]
    blocks, rows, columns = out.shape
    width = columns // 2
    me = block_of(meta, blocks)
    core = meta[0] & 1
    t = 0
    for own_ref, other_ref in zip(own1, other1, strict=True):
        for at in range(own_ref.shape[0]):
            own, other = own_ref[at, at1], other_ref[at, at1]
            real = jnp.where(core == 0, own, other)
            imag = jnp.where(core == 0, other, own)
            right[core, me ^ t, :, :width] = real
            right[core, me ^ t, :, width:] = imag
            right[1 - core, me ^ t, :, :width] = -imag
            right[1 - core, me ^ t, :, width:] = real
            t += 1
    left = jnp.concatenate([rows_of(own0, at0), rows_of(other0, at0)], axis=1)
    for at in range(columns // TILE):
        here = slice(at * TILE, (at + 1) * TILE)
        value = dot(left, right[:, :, :, here].reshape(columns, TILE))
        value = value.astype(bf16).reshape(blocks, rows, TILE)
        for t in range(blocks):
            out[me ^ t, :, here] = value[t]


def joined_right(chain, first, second):
    blocks, rows, width = first.blocks, first.rows, first.width
    return chain(
        functools.partial(joined_body, first.parts, first.at, second.at),
        shaped((blocks, rows, 2 * width)),
        [VMEM_SPEC] * (4 * first.parts),
        (*first.operands, *second.operands),
        [pltpu.VMEM((2, blocks, rows, 2 * width), bf16)],
        us=JOINED,
    )


def right_body(meta, stem, factor, out, both):
    count, columns = stem.shape
    width = columns // 2
    core = meta[0] & 1
    value = factor[...]
    both[:width] = value
    both[width:, :width] = -value[:, width:]
    both[width:, width:] = value[:, :width]
    left = stem[...]
    for at in range(columns // TILE):
        here = slice(at * TILE, (at + 1) * TILE)
        there = slice((at * TILE + width) % columns, (at * TILE + width) % columns + TILE)
        value = dot(left, both[:, here])
        turned = value if at * TILE < width else -value
        out[core, :, here] = value.astype(bf16)
        out[1 - core, :, there] = turned.astype(bf16)


def right_product(chain, stem, factor):
    count, columns = stem.shape
    return chain(
        right_body,
        shaped((2, count, columns)),
        [VMEM_SPEC] * 2,
        (stem, factor),
        [pltpu.VMEM((columns, columns), bf16)],
        us=RIGHT,
    )


def last_body(parts, at_branch, meta, *refs):
    own, other = refs[:parts], refs[parts : 2 * parts]
    right, out, wide, done, sems = refs[2 * parts :]
    blocks, rows, width = done.shape[0], done.shape[1] // 2, done.shape[2]
    total = blocks * rows
    me = block_of(meta, blocks)
    left = jnp.concatenate([rows_of(own, at_branch), rows_of(other, at_branch)], axis=1)
    target = out.reshape(blocks, 2 * rows, width)
    for at in range(width // TILE):
        for part in range(2):
            here = slice(part * width + at * TILE, part * width + (at + 1) * TILE)
            value = dot(left, right[:, :, here].reshape(2 * right.shape[1], TILE))
            for sub in range(TILE // 128):
                wide[at * (TILE // 128) + sub, pl.ds(part, total, stride=2), :] = value[:, sub * 128 : (sub + 1) * 128]
    writes = []
    for t in range(blocks):
        for at in range(width // 128):
            piece = wide[at, 2 * rows * t : 2 * rows * (t + 1), :]
            done[t, :, at * 128 : (at + 1) * 128] = piece.astype(bf16)
        writes.append(pltpu.make_async_copy(done.at[t], target.at[me ^ t], sems.at[t]))
        writes[-1].start()
    for copy in writes:
        copy.wait()


def last_product(chain, branch, right, shape):
    blocks, rows, width = branch.blocks, branch.rows, branch.width
    return chain(
        functools.partial(last_body, branch.parts, branch.at),
        shaped(shape),
        [VMEM_SPEC] * (2 * branch.parts + 1),
        (*branch.operands, right),
        [
            pltpu.VMEM((width // 128, 2 * blocks * rows, 128), f32),
            pltpu.VMEM((blocks, 2 * rows, width), bf16),
            pltpu.SemaphoreType.DMA((blocks,)),
        ],
        [ANY_SPEC],
        us=LAST,
    )


def exchange(x):
    return lax.all_to_all(x, "outer", split_axis=0, concat_axis=0, tiled=True)


class Sum:
    def __init__(self, chain, size, times, direct, keep, send):
        self.chain, self.size, self.times, self.direct = chain, size, times, direct
        self.levels = size.bit_length() - 1
        self.keep, self.recv = keep, self.swap(send, 0)

    def swap(self, x, shift):
        return swap_with(x, 1 << shift, self.size)

    def steps(self):
        levels, chain = self.levels, self.chain
        halve_us, spread_us, finish_us, join_us = self.times
        blocks = 1 << (levels - 2)
        rows = self.keep.shape[1] // (2 * blocks)
        keep, send = halve(chain, self.keep, self.recv, 1, halve_us)
        recv = self.swap(send, 1)
        yield
        if rows % 16 or not self.direct:
            for shift in range(2, levels):
                keep, send = halve(chain, keep, recv, shift, spread_us)
                recv = self.swap(send, shift)
                yield
            total = finish(chain, keep, [recv], finish_us)
            for shift in reversed(range(2, levels)):
                recv = self.swap(total, shift)
                yield
                total = join(chain, (total, recv), join_us)
        else:
            masks = [reversed_bits(t, levels - 2) << 2 for t in range(1, blocks)]
            keep, *sends = spread(chain, keep, recv, 2, blocks, spread_us)
            recvs = [swap_with(x, mask, self.size) for x, mask in zip(sends, masks, strict=True)]
            yield
            total = finish(chain, keep, recvs, finish_us)
            recvs = [swap_with(total, mask, self.size) for mask in masks]
            yield
            total = join(chain, (total, *recvs), join_us)
        across = self.swap(total, 1)
        self.own, self.other = (total, across), (self.swap(total, 0), self.swap(across, 0))
        if rows % 16:
            order = block_of(chain.meta, 2 * blocks) ^ jnp.arange(2 * blocks)
            self.own, self.other = (
                (jnp.swapaxes(jnp.concatenate(x, axis=0)[order], 0, 1).reshape(1, keep.shape[0], -1, keep.shape[2]),)
                for x in (self.own, self.other)
            )
        yield

    def result(self, at):
        return Summed(self.own, self.other, at)


def on_device(size, stem_tensor, leaf_left, leaf_right, slice_bits):
    width = stem_tensor.shape[1]
    place = lax.axis_index("outer").astype(jnp.int32)
    chain = Calls(jnp.concatenate([place[None], slice_bits.astype(jnp.int32)]))
    given = exchange(stem_tensor[0])
    early, late = ((0,),), ((1, 3), (2,))
    sums = [
        Sum(chain, size, times, direct, *parts)
        for times, direct, parts in zip(STEPS, DIRECT, leaf_partials(chain, leaf_left, leaf_right, early, LEAVES[0]))
    ]
    a = sums[0].steps()
    next(a, None)
    sums += [
        Sum(chain, size, times, direct, *parts)
        for times, direct, parts in zip(STEPS[1:], DIRECT[1:], leaf_partials(chain, leaf_left, leaf_right, late, LEAVES[1]))
    ]
    b, c = (total.steps() for total in sums[1:])
    next(a, None)
    next(b, None)
    next(c, None)
    right = prepare(chain, given)
    next(a, None)
    next(b, None)
    next(c, None)
    next(a, None)
    next(b, None)
    next(c, None)
    for _ in a:
        pass
    state = first_product(chain, sums[0].result(0), right).reshape(width, 2 * width)
    state = exchange(state)
    next(b, None)
    next(c, None)
    for steps in (b, c):
        for _ in steps:
            pass
    factor = joined_right(chain, sums[1].result(0), sums[1].result(1)).reshape(width, 2 * width)
    right = right_product(chain, state, factor)
    return last_product(chain, sums[2].result(0), right, stem_tensor.shape)


def solution(mesh):
    return jax.shard_map(
        functools.partial(on_device, mesh.shape["outer"]),
        mesh=mesh,
        in_specs=(
            P(("cuts", "outer"), None, None, None),
            P(None, None, "outer", None, None),
            P(None, None, "outer", None, None),
            P("cuts"),
        ),
        out_specs=P(("cuts", "outer"), None, None, None),
        check_vma=False,
    )
```

```python
import functools

import jax
import jax.numpy as jnp
from jax import lax
from jax.experimental import pallas as pl
from jax.experimental.pallas import tpu as pltpu
from jax.sharding import PartitionSpec as P

VMEM_LIMIT = 24 << 20
LEAF_LIMIT = 48 << 20
DIRECT = True, True, True
LEAVES = 0.1, 10.0
STEPS = (0.1, 20.0, 3.0, 10.0), (0.5, 20.0, 20.0, 20.0), (0.5, 5.0, 10.0, 20.0)
PREPARE, FIRST, JOINED, LAST = 0.1, 1.0, 2.0, 1.0
RIGHT = 2.0
TILE = 256
bf16, f32 = jnp.bfloat16, jnp.float32

SMEM_SPEC = pl.BlockSpec(memory_space=pltpu.SMEM)
VMEM_SPEC = pl.BlockSpec(memory_space=pltpu.VMEM)
ANY_SPEC = pl.BlockSpec(memory_space=pl.ANY)
HBM_SPEC = pl.BlockSpec(memory_space=pltpu.HBM)


class Calls:
    def __init__(self, meta):
        self.meta, self.last = meta, ()

    def __call__(self, body, shapes, in_specs, operands, scratch=(), out_specs=None, us=1.0, limit=VMEM_LIMIT):
        many = isinstance(shapes, (tuple, list))
        shapes = tuple(shapes) if many else (shapes,)
        after = self.last
        specs = [SMEM_SPEC] + list(in_specs) + [ANY_SPEC] * len(after)
        count = len(specs)

        def kernel(*refs):
            body(*refs[: len(in_specs) + 1], *refs[count:])

        out = pl.pallas_call(
            kernel,
            out_shape=shapes,
            in_specs=specs,
            out_specs=tuple(out_specs or [VMEM_SPEC] * len(shapes)),
            scratch_shapes=list(scratch),
            compiler_params=pltpu.CompilerParams(vmem_limit_bytes=limit),
            cost_estimate=pl.CostEstimate(flops=int(us * 1e9), bytes_accessed=1024, transcendentals=0),
        )(self.meta, *operands, *after)
        self.last = (out[0],)
        return out if many else out[0]


def shaped(shape, dtype=bf16):
    return jax.ShapeDtypeStruct(shape, dtype)


def tdot(a, b):
    return lax.dot_general(a, b, (((0,), (0,)), ((), ())), preferred_element_type=f32)


def dot(a, b):
    return jnp.dot(a, b, preferred_element_type=f32)


def reversed_bits(value, bits):
    found = 0
    for at in range(bits):
        found = found + ((value >> at) & 1) * (1 << (bits - 1 - at))
    return found


def block_of(meta, blocks):
    return reversed_bits(meta[0] >> 1, blocks.bit_length() - 1)


def leaf_body(groups, meta, left, right, *refs):
    outs, (lhs, rhs, both, sems) = refs[:-4], refs[-4:]
    depth, width = left.shape[2], left.shape[4]
    core = meta[0] & 1
    keep_at = pl.ds(pl.multiple_of(core * width, width), width)
    send_at = pl.ds(pl.multiple_of((1 - core) * width, width), width)
    branches = [branch for group in groups for branch in group]
    copies = []
    for at, branch in enumerate(branches):
        first, second = (right, left) if branch % 2 == 0 else (left, right)
        for which, (ref, buf) in enumerate(((second, rhs), (first, lhs))):
            flat = ref.reshape(ref.shape[0], ref.shape[1], 2 * depth, width)
            copies.append(
                pltpu.make_async_copy(flat.at[branch, meta[1 + branch]], buf.at[at], sems.at[at, which])
            )
            copies[-1].start()
    rows = lax.broadcasted_iota(jnp.int32, (2 * depth // 8, 8, width), 1)
    is_real = (rows & 1) == 0
    at = 0
    for group, keep, send in zip(groups, outs[0::2], outs[1::2], strict=True):
        for inside in range(len(group)):
            copies[2 * at].wait()
            wide = rhs[at].astype(f32).reshape(2 * depth // 8, 8, width)
            signed = jnp.where(is_real, wide, -wide)
            swapped = jnp.where(is_real, pltpu.roll(wide, 7, 1), pltpu.roll(wide, 1, 1))
            both[at % 2, :, keep_at] = signed.reshape(2 * depth, width).astype(bf16)
            both[at % 2, :, send_at] = swapped.reshape(2 * depth, width).astype(bf16)
            copies[2 * at + 1].wait()
            value = tdot(lhs[at], both[at % 2])
            keep[inside] = value[:, :width]
            send[inside] = value[:, width:].astype(bf16)
            at += 1


def leaf_partials(chain, left, right, groups, us):
    depth, width = left.shape[2], left.shape[4]
    count = sum(len(group) for group in groups)
    shapes = [shaped((len(group), width, width), dtype) for group in groups for dtype in (f32, bf16)]
    outs = chain(
        functools.partial(leaf_body, groups),
        shapes,
        [ANY_SPEC, ANY_SPEC],
        (left, right),
        [
            pltpu.VMEM((count, 2 * depth, width), bf16),
            pltpu.VMEM((count, 2 * depth, width), bf16),
            pltpu.VMEM((2, 2 * depth, 2 * width), bf16),
            pltpu.SemaphoreType.DMA((count, 2)),
        ],
        us=us,
        limit=LEAF_LIMIT,
    )
    return list(zip(outs[0::2], outs[1::2], strict=True))


def half_body(shift, meta, keep, recv, keep_out, send_out):
    half = keep_out.shape[1]
    bit = (meta[0] >> shift) & 1
    mine = pl.ds(pl.multiple_of(bit * half, half), half)
    other = pl.ds(pl.multiple_of((1 - bit) * half, half), half)
    send_out[...] = (keep[:, other] + recv[:, other].astype(f32)).astype(bf16)
    keep_out[...] = keep[:, mine] + recv[:, mine].astype(f32)


def halve(chain, keep, recv, shift, us):
    count, rows, width = keep.shape
    half = rows // 2
    if half % 16:
        total = (keep + recv.astype(f32)).reshape(count, 2, half, width)
        bit = (chain.meta[0] >> shift) & 1
        return total[:, bit], total[:, 1 - bit].astype(bf16)
    return chain(
        functools.partial(half_body, shift),
        (shaped((count, half, width), f32), shaped((count, half, width))),
        [VMEM_SPEC] * 2,
        (keep, recv),
        us=us,
    )


def spread_body(shift, meta, keep, recv, keep_out, *sends):
    rows = keep_out.shape[1]
    blocks = len(sends) + 1
    me = reversed_bits(meta[0] >> shift, blocks.bit_length() - 1)
    for t in range(blocks):
        at = pl.ds(pl.multiple_of((me ^ t) * rows, rows), rows)
        value = keep[:, at] + recv[:, at].astype(f32)
        if t:
            sends[t - 1][...] = value.astype(bf16)
        else:
            keep_out[...] = value


def spread(chain, keep, recv, shift, blocks, us):
    count, rows, width = keep.shape[0], keep.shape[1] // blocks, keep.shape[2]
    return chain(
        functools.partial(spread_body, shift),
        (shaped((count, rows, width), f32),) + (shaped((count, rows, width)),) * (blocks - 1),
        [VMEM_SPEC] * 2,
        (keep, recv),
        us=us,
    )


def finish_body(meta, keep, *rest):
    total = keep[...]
    for recv in rest[:-1]:
        total = total + recv[...].astype(f32)
    rest[-1][0] = total.astype(bf16)


def finish(chain, keep, recvs, us):
    if keep.shape[1] % 16:
        return (keep + sum(recv.astype(f32) for recv in recvs)).astype(bf16)[None]
    return chain(finish_body, shaped((1, *keep.shape)), [VMEM_SPEC] * (1 + len(recvs)), (keep, *recvs), us=us)


def join_body(meta, *refs):
    at = 0
    for ref in refs[:-1]:
        refs[-1][at : at + ref.shape[0]] = ref[...]
        at += ref.shape[0]


def join(chain, parts, us):
    blocks, shape = sum(part.shape[0] for part in parts), parts[0].shape[1:]
    if shape[1] % 16:
        return jnp.concatenate(parts, axis=0)
    return chain(join_body, shaped((blocks, *shape)), [VMEM_SPEC] * len(parts), parts, us=us)


def swap_with(x, mask, size):
    return lax.ppermute(x, "outer", [(i, i ^ mask) for i in range(size)])


def prepare_body(meta, stem, out, wide):
    count, width = stem.shape[0], stem.shape[2]
    core = meta[0] & 1
    flat = stem[...].reshape(2 * count, width)
    for at in range(width // 128):
        wide[at] = flat[:, at * 128 : (at + 1) * 128].astype(f32)
    for at in range(width // 128):
        here = slice(at * 128, (at + 1) * 128)
        there = slice(width + at * 128, width + (at + 1) * 128)
        real = wide[at, pl.ds(0, count, stride=2), :]
        imag = wide[at, pl.ds(1, count, stride=2), :]
        out[core, :, here] = real.astype(bf16)
        out[core, :, there] = imag.astype(bf16)
        out[1 - core, :, here] = (-imag).astype(bf16)
        out[1 - core, :, there] = real.astype(bf16)


def prepare(chain, stem):
    count, _, width = stem.shape
    return chain(
        prepare_body,
        shaped((2, count, 2 * width)),
        [VMEM_SPEC],
        (stem,),
        [pltpu.VMEM((width // 128, 2 * count, 128), f32)],
        us=PREPARE,
    )


class Summed:
    def __init__(self, own, other, at):
        self.own, self.other, self.at = own, other, at
        self.parts = len(own)
        self.blocks, (self.rows, self.width) = sum(part.shape[0] for part in own), own[0].shape[2:]
        self.operands = (*own, *other)


def rows_of(refs, at):
    return jnp.concatenate([ref[:, at].reshape(-1, ref.shape[3]) for ref in refs], axis=0)


def first_body(parts, at_branch, meta, *refs):
    own, other, (right, out) = refs[:parts], refs[parts : 2 * parts], refs[2 * parts :]
    blocks, rows, columns = out.shape
    me = block_of(meta, blocks)
    left = jnp.concatenate([rows_of(own, at_branch), rows_of(other, at_branch)], axis=1)
    for at in range(columns // TILE):
        here = slice(at * TILE, (at + 1) * TILE)
        value = dot(left, right[:, :, here].reshape(columns, TILE))
        value = value.astype(bf16).reshape(blocks, rows, TILE)
        for t in range(blocks):
            out[me ^ t, :, here] = value[t]


def first_product(chain, branch, right):
    return chain(
        functools.partial(first_body, branch.parts, branch.at),
        shaped((branch.blocks, branch.rows, 2 * branch.width)),
        [VMEM_SPEC] * (2 * branch.parts + 1),
        (*branch.operands, right),
        us=FIRST,
    )


def joined_body(parts, at0, at1, meta, *refs):
    own0, other0, own1, other1 = (refs[at * parts : (at + 1) * parts] for at in range(4))
    out, right = refs[4 * parts :]
    blocks, rows, columns = out.shape
    width = columns // 2
    me = block_of(meta, blocks)
    core = meta[0] & 1
    t = 0
    for own_ref, other_ref in zip(own1, other1, strict=True):
        for at in range(own_ref.shape[0]):
            own, other = own_ref[at, at1], other_ref[at, at1]
            real = jnp.where(core == 0, own, other)
            imag = jnp.where(core == 0, other, own)
            right[core, me ^ t, :, :width] = real
            right[core, me ^ t, :, width:] = imag
            right[1 - core, me ^ t, :, :width] = -imag
            right[1 - core, me ^ t, :, width:] = real
            t += 1
    left = jnp.concatenate([rows_of(own0, at0), rows_of(other0, at0)], axis=1)
    for at in range(columns // TILE):
        here = slice(at * TILE, (at + 1) * TILE)
        value = dot(left, right[:, :, :, here].reshape(columns, TILE))
        value = value.astype(bf16).reshape(blocks, rows, TILE)
        for t in range(blocks):
            out[me ^ t, :, here] = value[t]


def joined_right(chain, first, second):
    blocks, rows, width = first.blocks, first.rows, first.width
    return chain(
        functools.partial(joined_body, first.parts, first.at, second.at),
        shaped((blocks, rows, 2 * width)),
        [VMEM_SPEC] * (4 * first.parts),
        (*first.operands, *second.operands),
        [pltpu.VMEM((2, blocks, rows, 2 * width), bf16)],
        us=JOINED,
    )


def right_body(meta, stem, factor, out, both, sem):
    count, columns = stem.shape
    width = columns // 2
    core = meta[0] & 1
    copy = pltpu.make_async_copy(factor, both.at[pl.ds(0, width)], sem)
    copy.start()
    copy.wait()
    value = both[:width]
    both[width:, :width] = -value[:, width:]
    both[width:, width:] = value[:, :width]
    left = stem[...]
    for at in range(columns // TILE):
        here = slice(at * TILE, (at + 1) * TILE)
        there = slice((at * TILE + width) % columns, (at * TILE + width) % columns + TILE)
        value = dot(left, both[:, here])
        turned = value if at * TILE < width else -value
        out[core, :, here] = value.astype(bf16)
        out[1 - core, :, there] = turned.astype(bf16)


def right_product(chain, stem, factor):
    count, columns = stem.shape
    return chain(
        right_body,
        shaped((2, count, columns)),
        [VMEM_SPEC, HBM_SPEC],
        (stem, factor),
        [pltpu.VMEM((columns, columns), bf16), pltpu.SemaphoreType.DMA],
        us=RIGHT,
    )


def last_body(parts, at_branch, meta, *refs):
    own, other = refs[:parts], refs[parts : 2 * parts]
    right, out, wide, done, sems = refs[2 * parts :]
    blocks, rows, width = done.shape[0], done.shape[1] // 2, done.shape[2]
    total = blocks * rows
    me = block_of(meta, blocks)
    left = jnp.concatenate([rows_of(own, at_branch), rows_of(other, at_branch)], axis=1)
    target = out.reshape(blocks, 2 * rows, width)
    for at in range(width // TILE):
        for part in range(2):
            here = slice(part * width + at * TILE, part * width + (at + 1) * TILE)
            value = dot(left, right[:, :, here].reshape(2 * right.shape[1], TILE))
            for sub in range(TILE // 128):
                wide[at * (TILE // 128) + sub, pl.ds(part, total, stride=2), :] = value[:, sub * 128 : (sub + 1) * 128]
    writes = []
    for t in range(blocks):
        for at in range(width // 128):
            piece = wide[at, 2 * rows * t : 2 * rows * (t + 1), :]
            done[t, :, at * 128 : (at + 1) * 128] = piece.astype(bf16)
        writes.append(pltpu.make_async_copy(done.at[t], target.at[me ^ t], sems.at[t]))
        writes[-1].start()
    for copy in writes:
        copy.wait()


def last_product(chain, branch, right, shape):
    blocks, rows, width = branch.blocks, branch.rows, branch.width
    return chain(
        functools.partial(last_body, branch.parts, branch.at),
        shaped(shape),
        [VMEM_SPEC] * (2 * branch.parts + 1),
        (*branch.operands, right),
        [
            pltpu.VMEM((width // 128, 2 * blocks * rows, 128), f32),
            pltpu.VMEM((blocks, 2 * rows, width), bf16),
            pltpu.SemaphoreType.DMA((blocks,)),
        ],
        [ANY_SPEC],
        us=LAST,
    )


def exchange(x):
    return lax.all_to_all(x, "outer", split_axis=0, concat_axis=0, tiled=True)


class Sum:
    def __init__(self, chain, size, times, direct, keep, send):
        self.chain, self.size, self.times, self.direct = chain, size, times, direct
        self.levels = size.bit_length() - 1
        self.keep, self.recv = keep, self.swap(send, 0)

    def swap(self, x, shift):
        return swap_with(x, 1 << shift, self.size)

    def steps(self):
        levels, chain = self.levels, self.chain
        halve_us, spread_us, finish_us, join_us = self.times
        blocks = 1 << (levels - 2)
        rows = self.keep.shape[1] // (2 * blocks)
        keep, send = halve(chain, self.keep, self.recv, 1, halve_us)
        recv = self.swap(send, 1)
        yield
        if rows % 16 or not self.direct:
            for shift in range(2, levels):
                keep, send = halve(chain, keep, recv, shift, spread_us)
                recv = self.swap(send, shift)
                yield
            total = finish(chain, keep, [recv], finish_us)
            for shift in reversed(range(2, levels)):
                recv = self.swap(total, shift)
                yield
                total = join(chain, (total, recv), join_us)
        else:
            masks = [reversed_bits(t, levels - 2) << 2 for t in range(1, blocks)]
            keep, *sends = spread(chain, keep, recv, 2, blocks, spread_us)
            recvs = [swap_with(x, mask, self.size) for x, mask in zip(sends, masks, strict=True)]
            yield
            total = finish(chain, keep, recvs, finish_us)
            recvs = [swap_with(total, mask, self.size) for mask in masks]
            yield
            total = join(chain, (total, *recvs), join_us)
        across = self.swap(total, 1)
        self.own, self.other = (total, across), (self.swap(total, 0), self.swap(across, 0))
        if rows % 16:
            order = block_of(chain.meta, 2 * blocks) ^ jnp.arange(2 * blocks)
            self.own, self.other = (
                (jnp.swapaxes(jnp.concatenate(x, axis=0)[order], 0, 1).reshape(1, keep.shape[0], -1, keep.shape[2]),)
                for x in (self.own, self.other)
            )
        yield

    def result(self, at):
        return Summed(self.own, self.other, at)


def on_device(size, stem_tensor, leaf_left, leaf_right, slice_bits):
    width = stem_tensor.shape[1]
    place = lax.axis_index("outer").astype(jnp.int32)
    chain = Calls(jnp.concatenate([place[None], slice_bits.astype(jnp.int32)]))
    given = exchange(stem_tensor[0])
    early, late = ((0,),), ((1, 3), (2,))
    sums = [
        Sum(chain, size, times, direct, *parts)
        for times, direct, parts in zip(STEPS, DIRECT, leaf_partials(chain, leaf_left, leaf_right, early, LEAVES[0]))
    ]
    a = sums[0].steps()
    next(a, None)
    sums += [
        Sum(chain, size, times, direct, *parts)
        for times, direct, parts in zip(STEPS[1:], DIRECT[1:], leaf_partials(chain, leaf_left, leaf_right, late, LEAVES[1]))
    ]
    b, c = (total.steps() for total in sums[1:])
    next(a, None)
    next(b, None)
    next(c, None)
    right = prepare(chain, given)
    next(a, None)
    next(b, None)
    next(c, None)
    next(a, None)
    next(b, None)
    next(c, None)
    for _ in a:
        pass
    state = first_product(chain, sums[0].result(0), right).reshape(width, 2 * width)
    state = exchange(state)
    next(b, None)
    next(c, None)
    for steps in (b, c):
        for _ in steps:
            pass
    factor = joined_right(chain, sums[1].result(0), sums[1].result(1)).reshape(width, 2 * width)
    right = right_product(chain, state, factor)
    return last_product(chain, sums[2].result(0), right, stem_tensor.shape)


def solution(mesh):
    return jax.shard_map(
        functools.partial(on_device, mesh.shape["outer"]),
        mesh=mesh,
        in_specs=(
            P(("cuts", "outer"), None, None, None),
            P(None, None, "outer", None, None),
            P(None, None, "outer", None, None),
            P("cuts"),
        ),
        out_specs=P(("cuts", "outer"), None, None, None),
        check_vma=False,
    )
```
